256 devices in a mesh: ctx: 16 (over x, y_hi, core), tp: 16 (over y_lo, z).
Axes of the slice: x: 4, y: 4 (y_hi: 2, y_lo: 2; y = y_hi * 2 + y_lo), z: 8, core: 2. Of those that a mesh axis runs over, the one named last changes fastest.
Arguments:
- queries: bfloat16 [8192, 8192], P('ctx', 'tp'), may hold values from -5 to 5
- keys_values: bfloat16 [2, 8192, 1024], P(None, 'ctx'), may hold values from -5 to 5
- block_list: int32 [64, 16], P('ctx'), may hold values from -1 to 63, as said below
- out_weight: bfloat16 [8192, 8192], P('tp'), may hold values from -0.0625 to 0.0625
Outputs:
- projected: bfloat16 [8192, 8192], P('ctx', 'tp')
The draws below stay inside these ranges and needn't reach their ends.
Inputs may be any that keep to these rules, and one draw needn't show every extreme that they name: Row r of block_list names distinct key blocks, r first; after the listed blocks the remaining slots hold -1; the number listed tends to grow with r, and the last row lists 16.
All inputs are finite; a program needn't handle non-finite values.
Results may differ from the reference program's by a relative error of at most 0.023.
Values may be sent and summed in bfloat16 or wider, within the bound.
No kernel may reach another device: no remote copies, remote signals or barrier semaphores. Data moves between devices by JAX's collectives and lax.ppermute only.
A program may use at most 128 MiB of HBM per device.

```python
import jax
import jax.numpy as jnp
from jax import lax

D = 8192
HEADS = 64
KVH = 8
HD = 128
BLOCK = 128
KMAX = 16
TOKENS = 8192
N_TP = 16


def draw_queries(key, part):
    key = jax.random.fold_in(key, 11)
    nblk = TOKENS // BLOCK
    group = HEADS // KVH
    base = jnp.clip(jax.random.normal(key, (nblk, BLOCK, KVH, group, HD), jnp.float32), -5.0, 5.0)
    return base.reshape(TOKENS, HEADS * HD).astype(jnp.bfloat16)


def draw_keys_values(key, part):
    key = jax.random.fold_in(key, 23)
    nblk = TOKENS // BLOCK
    base = jnp.clip(jax.random.normal(key, (2, nblk, BLOCK, KVH * HD), jnp.float32), -5.0, 5.0)
    return base.reshape(2, TOKENS, KVH * HD).astype(jnp.bfloat16)


def draw_block_list(key, part):
    key = jax.random.fold_in(key, 37)
    nblk = TOKENS // BLOCK
    rows = jnp.arange(nblk, dtype=jnp.int32)
    count_key, perm_key = jax.random.split(key)
    reach = 1 + (KMAX - 1) * (rows + 1) // nblk
    drawn = jax.random.randint(count_key, (nblk,), 0, 1 << 20, dtype=jnp.int32) % (reach + 1)
    counts = jnp.minimum(1 + drawn, KMAX)
    counts = counts.at[nblk - 1].set(KMAX)

    def one_row(row):
        order = jax.random.permutation(jax.random.fold_in(perm_key, row), nblk - 1).astype(jnp.int32)
        others = (row + 1 + order) % nblk
        return jnp.concatenate([row[None], others[:KMAX - 1]])
    listed = jax.vmap(one_row)(rows)
    slots = jnp.arange(KMAX, dtype=jnp.int32)[None, :]
    return jnp.where(slots < counts[:, None], listed, -1).astype(jnp.int32)


def level_of(own_key, dims, cuts, least, top_value):
    gain = 1.0
    for axis_at, shards_of in cuts:
        heights = jax.random.uniform(jax.random.fold_in(jax.random.fold_in(own_key, 6), axis_at), (shards_of,), jnp.float32, least / len(cuts), top_value / len(cuts))
        gain = gain * jnp.repeat(jnp.exp(heights), dims[axis_at] // shards_of).reshape((-1,) + (1,) * (len(dims) - 1 - axis_at))
    return gain


def normal_values(stream_key, dims, scale, bound, cuts=(), held_as=jnp.bfloat16):
    entries = scale * jax.random.normal(stream_key, dims, jnp.float32)
    if cuts:
        entries = entries * level_of(stream_key, dims, cuts, -0.22, 0.18)
    return jnp.clip(entries, -bound, bound).astype(held_as)


def setup_inputs(seed: int = 0) -> dict:
    key_list = jax.random.split(jax.random.key(seed), 5)
    queries = draw_queries(jax.random.fold_in(key_list[4], 71), 0)
    keys_values = draw_keys_values(jax.random.fold_in(key_list[4], 71), 0)
    block_list = draw_block_list(jax.random.fold_in(key_list[4], 71), 0)
    out_weight = normal_values(key_list[3], (HEADS * HD, D), (HEADS * HD) ** -0.5, 0.0625, ((0, 16),))
    return {"queries": queries, "keys_values": keys_values, "block_list": block_list, "out_weight": out_weight}


def reference(queries, keys_values, block_list, out_weight):
    nblk = TOKENS // BLOCK
    group = HEADS // KVH
    scale = HD ** -0.5
    q_blocks = queries.reshape(nblk, BLOCK, KVH, group, HD)
    k_blocks = keys_values.reshape(2, nblk, BLOCK, KVH, HD)

    def one_block(pair):
        qblock, listed = pair
        valid = listed >= 0
        index = jnp.maximum(listed, 0).astype(jnp.int32)
        keys = k_blocks[0][index].astype(jnp.float32)
        vals = k_blocks[1][index].astype(jnp.float32)
        scores = jnp.einsum("bkgd,jckd->kgbjc", qblock.astype(jnp.float32), keys) * scale
        mask = valid[None, None, None, :, None]
        scores = jnp.where(mask, scores, -1e30)
        top = jnp.max(scores, axis=(3, 4), keepdims=True)
        weights = jnp.where(mask, jnp.exp(scores - top), 0.0)
        total = jnp.sum(weights, axis=(3, 4))
        rounded = lax.optimization_barrier(weights.astype(jnp.bfloat16)).astype(jnp.float32)
        summed = jnp.einsum("kgbjc,jckd->bkgd", rounded, vals)
        result = summed / jnp.transpose(total, (2, 0, 1))[..., None]
        return result.astype(jnp.bfloat16).reshape(BLOCK, HEADS * HD)

    attended = lax.map(one_block, (q_blocks, block_list)).reshape(TOKENS, HEADS * HD)
    width = HEADS * HD // N_TP
    att_groups = jnp.transpose(attended.reshape(TOKENS, N_TP, width), (1, 0, 2))
    weight_groups = out_weight.reshape(N_TP, width, D)

    def add_group(total, pair):
        part = jnp.dot(pair[0], pair[1], preferred_element_type=jnp.float32)
        part = lax.optimization_barrier(part.astype(jnp.bfloat16)).astype(jnp.float32)
        return total + part, None

    summed, _ = lax.scan(add_group, jnp.zeros((TOKENS, D), jnp.float32), (att_groups, weight_groups))
    return summed.astype(jnp.bfloat16)
```

```python
import functools
import math

import jax
import jax.numpy as jnp
from jax import lax
from jax.experimental import pallas as pl
from jax.experimental.pallas import tpu as pltpu
from jax.sharding import PartitionSpec as P

HD = 128
BLOCK = 128
KMAX = 16
GROUP = 4
AXES = ("ctx", "tp")
NX, NYH, NC, NYL, NZ = 4, 2, 2, 2, 8
SLOTS = NX * NYH * NC
SCALE2 = HD ** (-0.5) * math.log2(math.e)
CHUNKS = 2
LOW = -1e30


def pairs(move):
    out = []
    for x in range(NX):
        for y in range(4):
            for c in range(NC):
                for z in range(NZ):
                    x2, y2, c2, z2 = move(x, y, c, z)
                    x2, y2, c2, z2 = x2 % NX, y2 % 4, c2 % NC, z2 % NZ

                    def index(x, y, c, z):
                        return (x * 4 + (y // 2) * 2 + c) * 16 + (y % 2) * 8 + z

                    out.append((index(x, y, c, z), index(x2, y2, c2, z2)))
    return out


MOVES = {
    "x+": pairs(lambda x, y, c, z: (x + 1, y, c, z)),
    "x-": pairs(lambda x, y, c, z: (x - 1, y, c, z)),
    "z+": pairs(lambda x, y, c, z: (x, y, c, z + 1)),
    "z-": pairs(lambda x, y, c, z: (x, y, c, z - 1)),
    "core": pairs(lambda x, y, c, z: (x, y, c + 1, z)),
    "y_near": pairs(lambda x, y, c, z: (x, y ^ 1, c, z)),
    "y_far": pairs(lambda x, y, c, z: (x, 3 - y, c, z)),
}


def send(array, move):
    return lax.ppermute(array, AXES, MOVES[move])


def attention_kernel(blocks_here, counts, listed, q_ref, *refs):
    pieces = refs[:SLOTS]
    out_ref, kv, scores, top, total, acc, sems = refs[SLOTS:]
    copies = []
    for slot in range(SLOTS):
        copy = pltpu.make_async_copy(
            pieces[slot], kv.at[:, pl.ds(slot * 512, 512), :], sems.at[slot]
        )
        copy.start()
        copies.append(copy)
    for copy in copies:
        copy.wait()

    def block_of(row, j, count):
        j = jnp.minimum(j, count - 1)
        return pl.multiple_of(listed[row * KMAX + j] * BLOCK, BLOCK)

    def both(which, row, pair, count):
        one = block_of(row, 2 * pair, count)
        two = block_of(row, 2 * pair + 1, count)
        return jnp.concatenate([kv[which, pl.ds(one, BLOCK), :], kv[which, pl.ds(two, BLOCK), :]], 0)

    def one_row(row, carry):
        count = counts[row]
        n_pairs = (count + 1) // 2
        here = pl.ds(pl.multiple_of(row * BLOCK, BLOCK), BLOCK)
        q = jnp.concatenate([q_ref[here, g * HD : (g + 1) * HD] for g in range(GROUP)], 0)
        top[...] = jnp.full(top.shape, LOW, jnp.float32)

        def first(pair, inner):
            keys = both(0, row, pair, count)
            s = lax.dot_general(
                q, keys, (((1,), (1,)), ((), ())), preferred_element_type=jnp.float32
            )
            left = s[:, :BLOCK]
            right = jnp.where(2 * pair + 1 < count, s[:, BLOCK:], LOW)
            scores[pair, :, :BLOCK] = left
            scores[pair, :, BLOCK:] = right
            top[...] = jnp.maximum(top[...], jnp.maximum(left, right))
            return inner

        lax.fori_loop(0, n_pairs, first, 0)
        row_top = jnp.max(top[...], axis=1, keepdims=True) * SCALE2
        top[...] = jnp.broadcast_to(row_top, top.shape)
        total[...] = jnp.zeros(total.shape, jnp.float32)
        acc[...] = jnp.zeros(acc.shape, jnp.float32)

        def second(pair, inner):
            vals = both(1, row, pair, count)
            high = top[...]
            left = jnp.exp2(scores[pair, :, :BLOCK] * SCALE2 - high)
            right = jnp.exp2(scores[pair, :, BLOCK:] * SCALE2 - high)
            total[...] += left + right
            weights = jnp.concatenate([left.astype(jnp.bfloat16), right.astype(jnp.bfloat16)], 1)
            acc[...] += jnp.dot(weights, vals, preferred_element_type=jnp.float32)
            return inner

        lax.fori_loop(0, n_pairs, second, 0)
        result = (acc[...] / jnp.sum(total[...], axis=1, keepdims=True)).astype(jnp.bfloat16)
        for g in range(GROUP):
            out_ref[here, g * HD : (g + 1) * HD] = result[g * BLOCK : (g + 1) * BLOCK, :]
        return carry

    lax.fori_loop(0, blocks_here, one_row, 0)


def attention(counts, listed, q, pieces):
    tok, width = q.shape
    rows = GROUP * BLOCK
    smem = pl.BlockSpec(memory_space=pltpu.SMEM)
    vmem = pl.BlockSpec(memory_space=pltpu.VMEM)
    return pl.pallas_call(
        functools.partial(attention_kernel, tok // BLOCK),
        out_shape=jax.ShapeDtypeStruct((tok, width), jnp.bfloat16),
        in_specs=[smem, smem, vmem] + [pl.BlockSpec(memory_space=pl.ANY)] * SLOTS,
        out_specs=vmem,
        scratch_shapes=[
            pltpu.VMEM((2, SLOTS * 512, HD), jnp.bfloat16),
            pltpu.VMEM((KMAX // 2, rows, 2 * BLOCK), jnp.float32),
            pltpu.VMEM((rows, HD), jnp.float32),
            pltpu.VMEM((rows, HD), jnp.float32),
            pltpu.VMEM((rows, HD), jnp.float32),
            pltpu.SemaphoreType.DMA((SLOTS,)),
        ],
        compiler_params=pltpu.CompilerParams(vmem_limit_bytes=20 * 2**20),
        cost_estimate=pl.CostEstimate(
            flops=tok * 2048 * GROUP * HD * 8, bytes_accessed=6 * 2**20, transcendentals=tok * 2048 * 4
        ),
        name="attention",
    )(counts, listed, q, *pieces)


def project_kernel(n_recv, where, own_ref, near_ref, w_ref, w0a, w0b, w1a, w1b, *refs):
    recvs, out_ref = refs[:n_recv], refs[n_recv]
    mine = where[2] == 1
    value = jnp.dot(own_ref[...], w_ref[...], preferred_element_type=jnp.float32)
    half = near_ref.shape[1] // 2
    value += jnp.dot(
        near_ref[:, :half],
        jnp.where(mine, w0a[...], w0b[...]),
        preferred_element_type=jnp.float32,
    )
    value += jnp.dot(
        near_ref[:, half:],
        jnp.where(mine, w1a[...], w1b[...]),
        preferred_element_type=jnp.float32,
    )
    for recv in recvs:
        value += recv[...].astype(jnp.float32)
    out_ref[...] = value.astype(jnp.bfloat16)


def project(where, own, near, weights, parts, recvs):
    rows, depth = own.shape
    tile = 256
    n = 512 // tile
    grid_spec = pltpu.PrefetchScalarGridSpec(
        num_scalar_prefetch=1,
        grid=(n,),
        in_specs=[
            pl.BlockSpec((rows, depth), lambda j, w: (0, 0)),
            pl.BlockSpec((rows, depth), lambda j, w: (0, 0)),
            pl.BlockSpec((depth, tile), lambda j, w: (0, w[0] * n + j)),
        ]
        + [pl.BlockSpec((depth // 2, tile), lambda j, w: (0, w[1] * n + j))] * 4
        + [pl.BlockSpec((rows, tile), lambda j, w: (0, j))] * len(recvs),
        out_specs=pl.BlockSpec((rows, tile), lambda j, w: (0, j)),
    )
    return pl.pallas_call(
        functools.partial(project_kernel, len(recvs)),
        out_shape=jax.ShapeDtypeStruct((rows, 512), jnp.bfloat16),
        grid_spec=grid_spec,
        compiler_params=pltpu.CompilerParams(vmem_limit_bytes=12 * 2**20),
        cost_estimate=pl.CostEstimate(
            flops=2 * rows * 2 * depth * 512, bytes_accessed=3 * 2**20, transcendentals=0
        ),
        name="project",
    )(where, own, near, weights, *parts, *recvs)


def shards(queries, keys_values, block_list, out_weight):
    ctx = lax.axis_index("ctx")
    tp = lax.axis_index("tp")
    x, yh, c = ctx // 4, (ctx // 2) % 2, ctx % 2
    yl, z = tp // NZ, tp % NZ
    tok = queries.shape[0]
    width = queries.shape[1]

    head = yl * 4 + z // 2
    far_head = (1 - yl) * 4 + z // 2
    own = lax.dynamic_slice_in_dim(keys_values, head * HD, HD, 2)
    for_far = lax.dynamic_slice_in_dim(keys_values, far_head * HD, HD, 2)
    far = send(for_far, "y_far")
    from_left = send(own, "x+")
    from_right = send(own, "x-")

    half = NZ * 512
    quarter = half // 2

    def for_neighbour(link):
        return lax.dynamic_slice(
            out_weight, (link * 256, (1 - yl) * half + c * quarter), (256, quarter)
        )

    near_part = send(for_neighbour(0), "y_near")

    far_left = send(far, "x+")
    far_right = send(far, "x-")
    far_weight, _ = lax.optimization_barrier((for_neighbour(1), far))
    far_part = send(far_weight, "y_far")
    two_own = send(from_left, "x+")
    two_far = send(far_right, "x-")
    here = [own, far, from_right, far_right, two_own, two_far, from_left, far_left]
    there = [send(piece, "core") for piece in here]
    pieces = []
    for at in range(len(here)):
        pieces += [here[at], there[at]]
    near_other = send(near_part, "core")
    far_other = send(far_part, "core")
    parts = [near_part, near_other, far_part, far_other]

    shard = block_list // 4
    sx, sy, sc = shard // 4, (shard // 2) % 2, shard % 2
    slot = ((sx - x) % NX) * 4 + ((sy - yh) % 2) * 2 + (sc - c) % 2
    placed = jnp.where(block_list >= 0, slot * 4 + block_list % 4, 0).astype(jnp.int32)
    counts = jnp.sum((block_list >= 0).astype(jnp.int32), axis=1)

    rows = tok // CHUNKS
    per = rows // BLOCK
    attended, near = [], []
    for k in range(CHUNKS):
        done = attention(
            counts[k * per : (k + 1) * per],
            placed[k * per : (k + 1) * per].reshape(-1),
            queries[k * rows : (k + 1) * rows],
            pieces,
        )
        attended.append(done)
        near.append(send(done, "y_near"))

    def where(target):
        target = target % NZ
        return jnp.stack(
            [yl * NZ + target, target % 4, (target // 4 == c).astype(jnp.int32)]
        ).astype(jnp.int32)

    def step(k, target, recvs):
        return project(where(target), attended[k], near[k], out_weight, parts, recvs)

    up = [[] for _ in range(CHUNKS)]
    down = [[] for _ in range(CHUNKS)]
    for distance in (4, 3, 2, 1):
        for k in range(CHUNKS):
            if distance < 4 or k % 2 == 0:
                up[k] = [send(step(k, z + distance, up[k]), "z+")]
            if distance < 4 or k % 2 == 1:
                down[k] = [send(step(k, z - distance, down[k]), "z-")]
    results = [step(k, z, up[k] + down[k]) for k in range(CHUNKS)]
    return jnp.concatenate(results, 0)


def solution(mesh):
    in_specs = (P("ctx", "tp"), P(None, "ctx", None), P("ctx", None), P("tp", None))
    return jax.shard_map(
        shards, mesh=mesh, in_specs=in_specs, out_specs=P("ctx", "tp"), check_vma=False
    )
```

```python
import functools
import math

import jax
import jax.numpy as jnp
from jax import lax
from jax.experimental import pallas as pl
from jax.experimental.pallas import tpu as pltpu
from jax.sharding import PartitionSpec as P

HD = 128
BLOCK = 128
KMAX = 16
GROUP = 4
AXES = ("ctx", "tp")
NX, NYH, NC, NYL, NZ = 4, 2, 2, 2, 8
SLOTS = NX * NYH * NC
SCALE2 = HD ** (-0.5) * math.log2(math.e)
CHUNKS = 2
LOW = -1e30


def pairs(move):
    out = []
    for x in range(NX):
        for y in range(4):
            for c in range(NC):
                for z in range(NZ):
                    x2, y2, c2, z2 = move(x, y, c, z)
                    x2, y2, c2, z2 = x2 % NX, y2 % 4, c2 % NC, z2 % NZ

                    def index(x, y, c, z):
                        return (x * 4 + (y // 2) * 2 + c) * 16 + (y % 2) * 8 + z

                    out.append((index(x, y, c, z), index(x2, y2, c2, z2)))
    return out


MOVES = {
    "x+": pairs(lambda x, y, c, z: (x + 1, y, c, z)),
    "x-": pairs(lambda x, y, c, z: (x - 1, y, c, z)),
    "z+": pairs(lambda x, y, c, z: (x, y, c, z + 1)),
    "z-": pairs(lambda x, y, c, z: (x, y, c, z - 1)),
    "core": pairs(lambda x, y, c, z: (x, y, c + 1, z)),
    "y_near": pairs(lambda x, y, c, z: (x, y ^ 1, c, z)),
    "y_far": pairs(lambda x, y, c, z: (x, 3 - y, c, z)),
}


def send(array, move):
    return lax.ppermute(array, AXES, MOVES[move])


def attention_kernel(blocks_here, slots, counts, listed, q_ref, *refs):
    if slots:
        column, w_ref = refs[:2]
        pieces, refs = refs[2 : 2 + len(slots)], refs[2 + len(slots) :]
        out_ref, kv, wide_ref, scores, top, total, acc, sem = refs
        half = wide_ref.shape[1]
        start = pl.multiple_of(column[0] * half, half)
        fetch = pltpu.make_async_copy(w_ref.at[:, pl.ds(start, half)], wide_ref, sem)
        fetch.start()
        for piece, held in zip(pieces, slots):
            for at, slot in enumerate(held):
                value = piece[at] if len(held) > 1 else piece[...]
                kv[:, slot * 512 : (slot + 1) * 512, :] = value
    else:
        kv, out_ref, scores, top, total, acc = refs

    def block_of(row, j, count):
        j = jnp.minimum(j, count - 1)
        return pl.multiple_of(listed[row * KMAX + j] * BLOCK, BLOCK)

    def both(which, row, pair, count):
        one = block_of(row, 2 * pair, count)
        two = block_of(row, 2 * pair + 1, count)
        return jnp.concatenate([kv[which, pl.ds(one, BLOCK), :], kv[which, pl.ds(two, BLOCK), :]], 0)

    def one_row(row, carry):
        count = counts[row]
        n_pairs = (count + 1) // 2
        here = pl.ds(pl.multiple_of(row * BLOCK, BLOCK), BLOCK)
        q = jnp.concatenate([q_ref[here, g * HD : (g + 1) * HD] for g in range(GROUP)], 0)
        top[...] = jnp.full(top.shape, LOW, jnp.float32)

        def first(pair, inner):
            keys = both(0, row, pair, count)
            s = lax.dot_general(
                q, keys, (((1,), (1,)), ((), ())), preferred_element_type=jnp.float32
            )
            left = s[:, :BLOCK]
            right = jnp.where(2 * pair + 1 < count, s[:, BLOCK:], LOW)
            scores[pair, :, :BLOCK] = left
            scores[pair, :, BLOCK:] = right
            top[...] = jnp.maximum(top[...], jnp.maximum(left, right))
            return inner

        lax.fori_loop(0, n_pairs, first, 0)
        row_top = jnp.max(top[...], axis=1, keepdims=True) * SCALE2
        top[...] = jnp.broadcast_to(row_top, top.shape)
        total[...] = jnp.zeros(total.shape, jnp.float32)
        acc[...] = jnp.zeros(acc.shape, jnp.float32)

        def second(pair, inner):
            vals = both(1, row, pair, count)
            high = top[...]
            left = jnp.exp2(scores[pair, :, :BLOCK] * SCALE2 - high)
            right = jnp.exp2(scores[pair, :, BLOCK:] * SCALE2 - high)
            total[...] += left + right
            weights = jnp.concatenate([left.astype(jnp.bfloat16), right.astype(jnp.bfloat16)], 1)
            acc[...] += jnp.dot(weights, vals, preferred_element_type=jnp.float32)
            return inner

        lax.fori_loop(0, n_pairs, second, 0)
        result = (acc[...] / jnp.sum(total[...], axis=1, keepdims=True)).astype(jnp.bfloat16)
        for g in range(GROUP):
            out_ref[here, g * HD : (g + 1) * HD] = result[g * BLOCK : (g + 1) * BLOCK, :]
        return carry

    lax.fori_loop(0, blocks_here, one_row, 0)
    if slots:
        fetch.wait()


def attention(counts, listed, q, pieces, fetch=None):
    tok, width = q.shape
    rows = GROUP * BLOCK
    smem = pl.BlockSpec(memory_space=pltpu.SMEM)
    vmem = pl.BlockSpec(memory_space=pltpu.VMEM)
    out_shape = [jax.ShapeDtypeStruct((tok, width), jnp.bfloat16)]
    args, in_specs = [counts, listed, q], [smem, smem, vmem]
    scratch = [
        pltpu.VMEM((KMAX // 2, rows, 2 * BLOCK), jnp.float32),
        pltpu.VMEM((rows, HD), jnp.float32),
        pltpu.VMEM((rows, HD), jnp.float32),
        pltpu.VMEM((rows, HD), jnp.float32),
    ]
    slots = ()
    if fetch is not None:
        slots, column, weights = fetch
        args += [column, weights]
        in_specs += [smem, pl.BlockSpec(memory_space=pl.ANY)]
        depth, full = weights.shape
        out_shape.append(jax.ShapeDtypeStruct((2, SLOTS * 512, HD), jnp.bfloat16))
        out_shape.append(jax.ShapeDtypeStruct((depth, full // 2), jnp.bfloat16))
        scratch.append(pltpu.SemaphoreType.DMA)
    return pl.pallas_call(
        functools.partial(attention_kernel, tok // BLOCK, slots),
        out_shape=out_shape,
        in_specs=in_specs + [vmem] * len(pieces),
        out_specs=[vmem] * len(out_shape),
        scratch_shapes=scratch,
        compiler_params=pltpu.CompilerParams(vmem_limit_bytes=36 * 2**20),
        cost_estimate=pl.CostEstimate(
            flops=tok * 2048 * GROUP * HD * 8, bytes_accessed=6 * 2**20, transcendentals=tok * 2048 * 4
        ),
        name="attention",
    )(*args, *pieces)


def project_kernel(count, scalars, own_ref, near_ref, w_ref, w0a, w0b, w1a, w1b, *out_refs):
    core = scalars[0]
    half = near_ref.shape[1] // 2
    for i in range(count):
        target = scalars[1 + i]
        mine = target // 4 == core
        wide = pl.ds(pl.multiple_of(target * 512, 512), 512)
        part = pl.ds(pl.multiple_of((target % 4) * 512, 512), 512)
        value = jnp.dot(own_ref[...], w_ref[:, wide], preferred_element_type=jnp.float32)
        value += jnp.dot(
            near_ref[:, :half],
            jnp.where(mine, w0a[:, part], w0b[:, part]),
            preferred_element_type=jnp.float32,
        )
        value += jnp.dot(
            near_ref[:, half:],
            jnp.where(mine, w1a[:, part], w1b[:, part]),
            preferred_element_type=jnp.float32,
        )
        out_refs[i][...] = value.astype(jnp.bfloat16)


def project(core, targets, own, near, wide, parts):
    rows, depth = own.shape
    count = len(targets)
    smem = pl.BlockSpec(memory_space=pltpu.SMEM)
    vmem = pl.BlockSpec(memory_space=pltpu.VMEM)
    scalars = jnp.stack([core] + [t % NZ for t in targets]).astype(jnp.int32)
    return pl.pallas_call(
        functools.partial(project_kernel, count),
        out_shape=[jax.ShapeDtypeStruct((rows, 512), jnp.bfloat16)] * count,
        in_specs=[smem] + [vmem] * 7,
        out_specs=[vmem] * count,
        compiler_params=pltpu.CompilerParams(vmem_limit_bytes=36 * 2**20),
        cost_estimate=pl.CostEstimate(
            flops=2 * rows * 2 * depth * 512 * count, bytes_accessed=2**20 * count, transcendentals=0
        ),
        name="project",
    )(scalars, own, near, wide, *parts)


def shards(queries, keys_values, block_list, out_weight):
    ctx = lax.axis_index("ctx")
    tp = lax.axis_index("tp")
    x, yh, c = ctx // 4, (ctx // 2) % 2, ctx % 2
    yl, z = tp // NZ, tp % NZ
    tok = queries.shape[0]
    width = queries.shape[1]

    head = yl * 4 + z // 2
    far_head = (1 - yl) * 4 + z // 2
    own = lax.dynamic_slice_in_dim(keys_values, head * HD, HD, 2)
    for_far = lax.dynamic_slice_in_dim(keys_values, far_head * HD, HD, 2)
    far = send(for_far, "y_far")
    left = send(own, "x+")
    right = send(own, "x-")
    own_t = send(own, "core")

    half = NZ * 512
    quarter = half // 2

    def for_neighbour(weights, link):
        return lax.dynamic_slice(
            weights, (link * 256, (1 - yl) * half + c * quarter), (256, quarter)
        )

    weights_1, _ = lax.optimization_barrier((out_weight, own_t))
    near_part = send(for_neighbour(weights_1, 0), "y_near")

    far, left, right = lax.optimization_barrier((far, left, right))
    both = send(jnp.stack([far, left]), "x+")
    far_right = send(far, "x-")
    far_t, left_t, right_t = send(far, "core"), send(left, "core"), send(right, "core")
    weights_2, _ = lax.optimization_barrier((out_weight, far_t))
    far_part = send(for_neighbour(weights_2, 1), "y_far")
    two_far = send(far_right, "x-")
    far_right_t = send(far_right, "core")
    both_t = send(both, "core")
    two_far_t = send(two_far, "core")
    near_other = send(near_part, "core")
    far_other = send(far_part, "core")
    parts = [near_part, near_other, far_part, far_other]
    pieces = [own, own_t, far, far_t, right, right_t, far_right, far_right_t]
    pieces += [two_far, two_far_t, left, left_t, both, both_t]
    slots = ((0,), (1,), (2,), (3,), (4,), (5,), (6,), (7,))
    slots += ((10,), (11,), (12,), (13,), (14, 8), (15, 9))

    shard = block_list // 4
    sx, sy, sc = shard // 4, (shard // 2) % 2, shard % 2
    slot = ((sx - x) % NX) * 4 + ((sy - yh) % 2) * 2 + (sc - c) % 2
    placed = jnp.where(block_list >= 0, slot * 4 + block_list % 4, 0).astype(jnp.int32)
    counts = jnp.sum((block_list >= 0).astype(jnp.int32), axis=1)

    rows = tok // CHUNKS
    per = rows // BLOCK

    def attend(k, *rest):
        return attention(
            counts[k * per : (k + 1) * per],
            placed[k * per : (k + 1) * per].reshape(-1),
            queries[k * rows : (k + 1) * rows],
            *rest,
        )

    first, kv, wide = attend(0, pieces, (slots, yl.reshape(1), out_weight))
    attended = [first] + [attend(k, [kv])[0] for k in range(1, CHUNKS)]
    near = [send(done, "y_near") for done in attended]

    ways = []
    for k in range(CHUNKS):
        up, down = ((4, 3, 2, 1), (-3, -2, -1)) if k % 2 == 0 else ((3, 2, 1), (-4, -3, -2, -1))
        early = [up[0], down[0]]
        late = [*up[1:], *down[1:], 0]
        partial = {}
        for group in (early, late):
            done = project(c, [z + d for d in group], attended[k], near[k], wide, parts)
            partial.update(zip(group, done))
        ways.append((up, down, partial))

    def add(*terms):
        return sum(t.astype(jnp.float32) for t in terms).astype(jnp.bfloat16)

    moving = [[None, None] for _ in range(CHUNKS)]
    for step in range(4):
        for k in range(CHUNKS):
            up, down, partial = ways[k]
            for way, (order, move) in enumerate(((up, "z+"), (down, "z-"))):
                if step < len(order):
                    value = partial[order[step]]
                    if step:
                        value = add(moving[k][way], value)
                    moving[k][way] = send(value, move)
    results = [add(ways[k][2][0], *moving[k]) for k in range(CHUNKS)]
    return jnp.concatenate(results, 0)


def solution(mesh):
    in_specs = (P("ctx", "tp"), P(None, "ctx", None), P("ctx", None), P("tp", None))
    return jax.shard_map(
        shards, mesh=mesh, in_specs=in_specs, out_specs=P("ctx", "tp"), check_vma=False
    )
```

```python
import functools
import math

import jax
import jax.numpy as jnp
from jax import lax
from jax.experimental import pallas as pl
from jax.experimental.pallas import tpu as pltpu
from jax.sharding import PartitionSpec as P

HD = 128
BLOCK = 128
KMAX = 16
GROUP = 4
AXES = ("ctx", "tp")
NX, NYH, NC, NYL, NZ = 4, 2, 2, 2, 8
SLOTS = NX * NYH * NC
SCALE2 = HD ** (-0.5) * math.log2(math.e)
CHUNKS = 2
LOW = -1e30
VMEM_LIMIT = 60 * 2**20
FREE = pl.CostEstimate(flops=0, bytes_accessed=0, transcendentals=0)


def pairs(move):
    out = []
    for x in range(NX):
        for y in range(4):
            for c in range(NC):
                for z in range(NZ):
                    x2, y2, c2, z2 = move(x, y, c, z)
                    x2, y2, c2, z2 = x2 % NX, y2 % 4, c2 % NC, z2 % NZ

                    def index(x, y, c, z):
                        return (x * 4 + (y // 2) * 2 + c) * 16 + (y % 2) * 8 + z

                    out.append((index(x, y, c, z), index(x2, y2, c2, z2)))
    return out


MOVES = {
    "x+": pairs(lambda x, y, c, z: (x + 1, y, c, z)),
    "x-": pairs(lambda x, y, c, z: (x - 1, y, c, z)),
    "z+": pairs(lambda x, y, c, z: (x, y, c, z + 1)),
    "z-": pairs(lambda x, y, c, z: (x, y, c, z - 1)),
    "core": pairs(lambda x, y, c, z: (x, y, c + 1, z)),
    "y_near": pairs(lambda x, y, c, z: (x, y ^ 1, c, z)),
    "y_far": pairs(lambda x, y, c, z: (x, 3 - y, c, z)),
}


def send(array, move):
    return lax.ppermute(array, AXES, MOVES[move])


SMEM = pl.BlockSpec(memory_space=pltpu.SMEM)
VMEM = pl.BlockSpec(memory_space=pltpu.VMEM)
HBM = pl.BlockSpec(memory_space=pltpu.HBM)


def pick_kernel(at, kv_ref, w_ref, own_ref, far_ref, near_w_ref, far_w_ref, sems):
    def lanes(i, n):
        return pl.ds(pl.multiple_of(at[i] * n, n), n)

    rows, columns = near_w_ref.shape
    copies = [
        pltpu.make_async_copy(kv_ref.at[:, :, lanes(0, HD)], own_ref, sems.at[0]),
        pltpu.make_async_copy(kv_ref.at[:, :, lanes(1, HD)], far_ref, sems.at[1]),
        pltpu.make_async_copy(w_ref.at[pl.ds(0, rows), lanes(2, columns)], near_w_ref, sems.at[2]),
        pltpu.make_async_copy(w_ref.at[pl.ds(rows, rows), lanes(2, columns)], far_w_ref, sems.at[3]),
    ]
    for copy in copies:
        copy.start()
    for copy in copies:
        copy.wait()


def pick(at, keys_values, weights):
    two, tok, _ = keys_values.shape
    depth, full = weights.shape
    piece = jax.ShapeDtypeStruct((two, tok, HD), jnp.bfloat16)
    part = jax.ShapeDtypeStruct((depth // 2, full // 4), jnp.bfloat16)
    return pl.pallas_call(
        pick_kernel,
        out_shape=[piece, piece, part, part],
        in_specs=[SMEM, HBM, HBM],
        out_specs=[HBM] * 4,
        scratch_shapes=[pltpu.SemaphoreType.DMA((4,))],
        compiler_params=pltpu.CompilerParams(vmem_limit_bytes=VMEM_LIMIT),
        cost_estimate=FREE,
        name="pick",
    )(at, keys_values, weights)


def attention_kernel(blocks_here, slots, counts, listed, q_ref, *refs):
    pieces, refs = refs[: len(slots)], refs[len(slots) :]
    out_ref, kv, scores, top, total, acc, sems = refs
    copies = []
    for piece, held in zip(pieces, slots):
        for at, slot in enumerate(held):
            source = piece.at[at] if len(held) > 1 else piece
            copies.append(
                pltpu.make_async_copy(source, kv.at[:, pl.ds(slot * 512, 512), :], sems.at[slot])
            )
    for copy in copies:
        copy.start()
    for copy in copies:
        copy.wait()

    def block_of(row, j, count):
        j = jnp.minimum(j, count - 1)
        return pl.multiple_of(listed[row * KMAX + j] * BLOCK, BLOCK)

    def both(which, row, pair, count):
        one = block_of(row, 2 * pair, count)
        two = block_of(row, 2 * pair + 1, count)
        return jnp.concatenate([kv[which, pl.ds(one, BLOCK), :], kv[which, pl.ds(two, BLOCK), :]], 0)

    def one_row(row, carry):
        count = counts[row]
        n_pairs = (count + 1) // 2
        here = pl.ds(pl.multiple_of(row * BLOCK, BLOCK), BLOCK)
        q = jnp.concatenate([q_ref[here, g * HD : (g + 1) * HD] for g in range(GROUP)], 0)
        top[...] = jnp.full(top.shape, LOW, jnp.float32)

        def first(pair, inner):
            keys = both(0, row, pair, count)
            s = lax.dot_general(
                q, keys, (((1,), (1,)), ((), ())), preferred_element_type=jnp.float32
            )
            left = s[:, :BLOCK]
            right = jnp.where(2 * pair + 1 < count, s[:, BLOCK:], LOW)
            scores[pair, :, :BLOCK] = left
            scores[pair, :, BLOCK:] = right
            top[...] = jnp.maximum(top[...], jnp.maximum(left, right))
            return inner

        lax.fori_loop(0, n_pairs, first, 0)
        row_top = jnp.max(top[...], axis=1, keepdims=True) * SCALE2
        top[...] = jnp.broadcast_to(row_top, top.shape)
        total[...] = jnp.zeros(total.shape, jnp.float32)
        acc[...] = jnp.zeros(acc.shape, jnp.float32)

        def second(pair, inner):
            vals = both(1, row, pair, count)
            high = top[...]
            left = jnp.exp2(scores[pair, :, :BLOCK] * SCALE2 - high)
            right = jnp.exp2(scores[pair, :, BLOCK:] * SCALE2 - high)
            total[...] += left + right
            weights = jnp.concatenate([left.astype(jnp.bfloat16), right.astype(jnp.bfloat16)], 1)
            acc[...] += jnp.dot(weights, vals, preferred_element_type=jnp.float32)
            return inner

        lax.fori_loop(0, n_pairs, second, 0)
        result = (acc[...] / jnp.sum(total[...], axis=1, keepdims=True)).astype(jnp.bfloat16)
        for g in range(GROUP):
            out_ref[here, g * HD : (g + 1) * HD] = result[g * BLOCK : (g + 1) * BLOCK, :]
        return carry

    lax.fori_loop(0, blocks_here, one_row, 0)


def attention(counts, listed, q, pieces, slots):
    tok, width = q.shape
    rows = GROUP * BLOCK
    return pl.pallas_call(
        functools.partial(attention_kernel, tok // BLOCK, slots),
        out_shape=jax.ShapeDtypeStruct((tok, width), jnp.bfloat16),
        in_specs=[SMEM, SMEM, VMEM] + [HBM] * len(pieces),
        out_specs=VMEM,
        scratch_shapes=[
            pltpu.VMEM((2, SLOTS * 512, HD), jnp.bfloat16),
            pltpu.VMEM((KMAX // 2, rows, 2 * BLOCK), jnp.float32),
            pltpu.VMEM((rows, HD), jnp.float32),
            pltpu.VMEM((rows, HD), jnp.float32),
            pltpu.VMEM((rows, HD), jnp.float32),
            pltpu.SemaphoreType.DMA((SLOTS,)),
        ],
        compiler_params=pltpu.CompilerParams(vmem_limit_bytes=VMEM_LIMIT),
        cost_estimate=FREE,
        name="attention",
    )(counts, listed, q, *pieces)


def project_kernel(count, scalars, own_ref, near_ref, w_ref, w0a, w0b, w1a, w1b, *refs):
    out_refs, (wide, sems, part_sems) = refs[:count], refs[count:]
    core, column = scalars[0], scalars[1]
    depth = own_ref.shape[1]
    half = depth // 2

    def lanes(block):
        return pl.ds(pl.multiple_of(block * 512, 512), 512)

    def own_copy(i, target):
        return pltpu.make_async_copy(
            w_ref.at[:, lanes(column * NZ + target)], wide.at[i, pl.ds(0, depth), :], sems.at[i]
        )

    def part_copy(i, target, which, source):
        return pltpu.make_async_copy(
            source.at[:, lanes(target % 4)],
            wide.at[i, pl.ds(depth + which * half, half), :],
            part_sems.at[i, which],
        )

    for i in range(count):
        target = scalars[2 + i]
        own_copy(i, target).start()

        @pl.when(target // 4 == core)
        def _():
            part_copy(i, target, 0, w0a).start()
            part_copy(i, target, 1, w1a).start()

        @pl.when(target // 4 != core)
        def _():
            part_copy(i, target, 0, w0b).start()
            part_copy(i, target, 1, w1b).start()

    for i in range(count):
        target = scalars[2 + i]
        own_copy(i, target).wait()
        part_copy(i, target, 0, w0a).wait()
        part_copy(i, target, 1, w1a).wait()
        value = jnp.dot(own_ref[...], wide[i, :depth, :], preferred_element_type=jnp.float32)
        value += jnp.dot(near_ref[...], wide[i, depth:, :], preferred_element_type=jnp.float32)
        out_refs[i][...] = value.astype(jnp.bfloat16)


def project(core, column, targets, own, near, weights, parts):
    rows, depth = own.shape
    count = len(targets)
    scalars = jnp.stack([core, column] + [t % NZ for t in targets]).astype(jnp.int32)
    return pl.pallas_call(
        functools.partial(project_kernel, count),
        out_shape=[jax.ShapeDtypeStruct((rows, 512), jnp.bfloat16)] * count,
        in_specs=[SMEM, VMEM, VMEM] + [HBM] * 5,
        out_specs=[VMEM] * count,
        scratch_shapes=[
            pltpu.VMEM((count, 2 * depth, 512), jnp.bfloat16),
            pltpu.SemaphoreType.DMA((count,)),
            pltpu.SemaphoreType.DMA((count, 2)),
        ],
        compiler_params=pltpu.CompilerParams(vmem_limit_bytes=VMEM_LIMIT),
        cost_estimate=FREE,
        name="project",
    )(scalars, own, near, weights, *parts)


def shards(queries, keys_values, block_list, out_weight):
    ctx = lax.axis_index("ctx")
    tp = lax.axis_index("tp")
    x, yh, c = ctx // 4, (ctx // 2) % 2, ctx % 2
    yl, z = tp // NZ, tp % NZ
    tok = queries.shape[0]
    width = queries.shape[1]

    head = yl * 4 + z // 2
    far_head = (1 - yl) * 4 + z // 2
    at = jnp.stack([head, far_head, (1 - yl) * 2 + c]).astype(jnp.int32)
    own, for_far, near_w, far_w = pick(at, keys_values, out_weight)
    far = send(for_far, "y_far")
    left = send(own, "x+")
    right = send(own, "x-")
    own_t = send(own, "core")
    near_part = send(near_w, "y_near")

    far, left, right, far_w = lax.optimization_barrier((far, left, right, far_w))
    first = jnp.stack([far, left])
    both = send(first, "x+")
    far_right = send(far, "x-")
    first_t = send(first, "core")
    right_t = send(right, "core")
    far_part = send(far_w, "y_far")
    two_far = send(far_right, "x-")
    far_right_t = send(far_right, "core")
    both_t = send(both, "core")
    two_far_t = send(two_far, "core")
    near_other = send(near_part, "core")
    far_other = send(far_part, "core")
    parts = [near_part, near_other, far_part, far_other]
    pieces = [own, own_t, first, first_t, right, right_t, far_right, far_right_t]
    pieces += [two_far, two_far_t, both, both_t]
    slots = ((0,), (1,), (2, 12), (3, 13), (4,), (5,), (6,), (7,))
    slots += ((10,), (11,), (14, 8), (15, 9))

    shard = block_list // 4
    sx, sy, sc = shard // 4, (shard // 2) % 2, shard % 2
    slot = ((sx - x) % NX) * 4 + ((sy - yh) % 2) * 2 + (sc - c) % 2
    placed = jnp.where(block_list >= 0, slot * 4 + block_list % 4, 0).astype(jnp.int32)
    counts = jnp.sum((block_list >= 0).astype(jnp.int32), axis=1)

    rows = tok // CHUNKS
    per = rows // BLOCK

    def attend(k):
        return attention(
            counts[k * per : (k + 1) * per],
            placed[k * per : (k + 1) * per].reshape(-1),
            queries[k * rows : (k + 1) * rows],
            pieces,
            slots,
        )

    attended = [attend(k) for k in range(CHUNKS)]
    near = [send(done, "y_near") for done in attended]

    ways = []
    for k in range(CHUNKS):
        up, down = ((4, 3, 2, 1), (-3, -2, -1)) if k % 2 == 0 else ((3, 2, 1), (-4, -3, -2, -1))
        early = [up[0], down[0]]
        late = [*up[1:], *down[1:], 0]
        partial = {}
        for group in (early, late):
            done = project(c, yl, [z + d for d in group], attended[k], near[k], out_weight, parts)
            partial.update(zip(group, done))
            if group is early and k + 1 < CHUNKS:
                near[k + 1], partial[up[0]], partial[down[0]] = lax.optimization_barrier(
                    (near[k + 1], partial[up[0]], partial[down[0]])
                )
        ways.append((up, down, partial))

    def add(*terms):
        return sum(t.astype(jnp.float32) for t in terms).astype(jnp.bfloat16)

    moving = [[None, None] for _ in range(CHUNKS)]
    for step in range(4):
        for k in range(CHUNKS):
            up, down, partial = ways[k]
            for way, (order, move) in enumerate(((up, "z+"), (down, "z-"))):
                if step < len(order):
                    value = partial[order[step]]
                    if step:
                        value = add(moving[k][way], value)
                    moving[k][way] = send(value, move)
    results = [add(ways[k][2][0], *moving[k]) for k in range(CHUNKS)]
    return jnp.concatenate(results, 0)


def solution(mesh):
    in_specs = (P("ctx", "tp"), P(None, "ctx", None), P("ctx", None), P("tp", None))
    return jax.shard_map(
        shards, mesh=mesh, in_specs=in_specs, out_specs=P("ctx", "tp"), check_vma=False
    )
```

```python
import functools
import math

import jax
import jax.numpy as jnp
from jax import lax
from jax.experimental import pallas as pl
from jax.experimental.pallas import tpu as pltpu
from jax.sharding import PartitionSpec as P

HD = 128
BLOCK = 128
KMAX = 16
GROUP = 4
AXES = ("ctx", "tp")
NX, NYH, NC, NYL, NZ = 4, 2, 2, 2, 8
SLOTS = NX * NYH * NC
SCALE2 = HD ** (-0.5) * math.log2(math.e)
CHUNKS = 2
LOW = -1e30
NEAR_ROWS = 256
ATTENTION_VMEM = 14 * 2**20
PROJECT_VMEM = 8 * 2**20
WIDE = 4
ATT_FLOPS = 3_000_000_000
VMEM_LIMIT = 50 * 2**20
FREE = pl.CostEstimate(flops=0, bytes_accessed=0, transcendentals=0)


def pairs(move):
    out = []
    for x in range(NX):
        for y in range(4):
            for c in range(NC):
                for z in range(NZ):
                    x2, y2, c2, z2 = move(x, y, c, z)
                    x2, y2, c2, z2 = x2 % NX, y2 % 4, c2 % NC, z2 % NZ

                    def index(x, y, c, z):
                        return (x * 4 + (y // 2) * 2 + c) * 16 + (y % 2) * 8 + z

                    out.append((index(x, y, c, z), index(x2, y2, c2, z2)))
    return out


MOVES = {
    "x+": pairs(lambda x, y, c, z: (x + 1, y, c, z)),
    "x-": pairs(lambda x, y, c, z: (x - 1, y, c, z)),
    "z+": pairs(lambda x, y, c, z: (x, y, c, z + 1)),
    "z-": pairs(lambda x, y, c, z: (x, y, c, z - 1)),
    "core": pairs(lambda x, y, c, z: (x, y, c + 1, z)),
    "y_near": pairs(lambda x, y, c, z: (x, y ^ 1, c, z)),
    "y_far": pairs(lambda x, y, c, z: (x, 3 - y, c, z)),
}


def send(array, move):
    return lax.ppermute(array, AXES, MOVES[move])


SMEM = pl.BlockSpec(memory_space=pltpu.SMEM)
VMEM = pl.BlockSpec(memory_space=pltpu.VMEM)
HBM = pl.BlockSpec(memory_space=pltpu.HBM)


def pick_kernel(coords, w_ref, near_w_ref, far_w_ref, sems):
    c, yl = coords[2], coords[3]
    columns = near_w_ref.shape[1]
    near_rows, far_rows = near_w_ref.shape[0], far_w_ref.shape[0]
    there = pl.ds(pl.multiple_of(((1 - yl) * 2 + c) * columns, columns), columns)
    copies = [
        pltpu.make_async_copy(w_ref.at[pl.ds(0, near_rows), there], near_w_ref, sems.at[0]),
        pltpu.make_async_copy(w_ref.at[pl.ds(near_rows, far_rows), there], far_w_ref, sems.at[1]),
    ]
    for copy in copies:
        copy.start()
    for copy in copies:
        copy.wait()


def pick(coords, weights):
    depth, full = weights.shape
    parts = [jax.ShapeDtypeStruct((n, full // 4), jnp.bfloat16) for n in (NEAR_ROWS, depth - NEAR_ROWS)]
    return pl.pallas_call(
        pick_kernel,
        out_shape=parts,
        in_specs=[SMEM, HBM],
        out_specs=[VMEM] * 2,
        scratch_shapes=[pltpu.SemaphoreType.DMA((2,))],
        compiler_params=pltpu.CompilerParams(vmem_limit_bytes=VMEM_LIMIT),
        cost_estimate=FREE,
        name="pick",
    )(coords, weights)


def attention_kernel(first_row, n_rows, slots, coords, block_list, q_ref, *refs):
    pieces, refs = refs[: len(slots)], refs[len(slots) :]
    out_ref, kv, scores, top, total, acc, placed = refs
    x, yh, c = coords[0], coords[1], coords[2]

    for piece, held in zip(pieces, slots):
        for i, slot in enumerate(held):
            kv[:, slot * 512 : (slot + 1) * 512, :] = piece[i] if len(held) > 1 else piece[...]

    counts = []
    for row in range(n_rows):

        def place(j, count):
            block = block_list[first_row + row, j]
            shard = jnp.maximum(block, 0) // 4
            slot = ((shard // 4 - x) % NX) * 4 + (((shard // 2) % 2 - yh) % 2) * 2 + (shard - c) % 2
            placed[row, j] = (slot * 4 + block % 4) * BLOCK
            return count + (block >= 0).astype(jnp.int32)

        counts.append(lax.fori_loop(0, KMAX, place, 0))

    for row in range(n_rows):
        count = counts[row]
        groups = (count + WIDE - 1) // WIDE

        def gather(which, group):
            tiles = []
            for i in range(WIDE):
                j = jnp.minimum(group * WIDE + i, count - 1)
                tiles.append(kv[which, pl.ds(pl.multiple_of(placed[row, j], BLOCK), BLOCK), :])
            return jnp.concatenate(tiles, 0)

        here = slice(row * BLOCK, (row + 1) * BLOCK)
        rows = slice((first_row + row) * BLOCK, (first_row + row + 1) * BLOCK)
        q = jnp.concatenate([q_ref[rows, g * HD : (g + 1) * HD] for g in range(GROUP)], 0)
        top[...] = jnp.full(top.shape, LOW, jnp.float32)

        def first(group, carry):
            s = lax.dot_general(
                q, gather(0, group), (((1,), (1,)), ((), ())), preferred_element_type=jnp.float32
            )
            high = top[...]
            for i in range(WIDE):
                tile = s[:, i * BLOCK : (i + 1) * BLOCK]
                if i:
                    tile = jnp.where(group * WIDE + i < count, tile, LOW)
                scores[group, :, i * BLOCK : (i + 1) * BLOCK] = tile
                high = jnp.maximum(high, tile)
            top[...] = high
            return carry

        lax.fori_loop(0, groups, first, 0)
        top[...] = jnp.broadcast_to(jnp.max(top[...], axis=1, keepdims=True) * SCALE2, top.shape)
        total[...] = jnp.zeros(total.shape, jnp.float32)
        acc[...] = jnp.zeros(acc.shape, jnp.float32)

        def second(group, carry):
            high = top[...]
            added, weights = total[...], []
            for i in range(WIDE):
                tile = jnp.exp2(scores[group, :, i * BLOCK : (i + 1) * BLOCK] * SCALE2 - high)
                added += tile
                weights.append(tile.astype(jnp.bfloat16))
            total[...] = added
            acc[...] += jnp.dot(
                jnp.concatenate(weights, 1), gather(1, group), preferred_element_type=jnp.float32
            )
            return carry

        lax.fori_loop(0, groups, second, 0)
        result = (acc[...] / jnp.sum(total[...], axis=1, keepdims=True)).astype(jnp.bfloat16)
        for g in range(GROUP):
            out_ref[here, g * HD : (g + 1) * HD] = result[g * BLOCK : (g + 1) * BLOCK, :]


def attention(coords, block_list, q, first_row, n_rows, pieces, slots):
    rows = GROUP * BLOCK
    tok, width = n_rows * BLOCK, q.shape[1]
    return pl.pallas_call(
        functools.partial(attention_kernel, first_row, n_rows, slots),
        out_shape=jax.ShapeDtypeStruct((tok, width), jnp.bfloat16),
        in_specs=[SMEM, SMEM, VMEM] + [VMEM] * len(pieces),
        out_specs=VMEM,
        scratch_shapes=[
            pltpu.VMEM((2, SLOTS * 512, HD), jnp.bfloat16),
            pltpu.VMEM((KMAX // WIDE, rows, WIDE * BLOCK), jnp.float32),
            pltpu.VMEM((rows, HD), jnp.float32),
            pltpu.VMEM((rows, HD), jnp.float32),
            pltpu.VMEM((rows, HD), jnp.float32),
            pltpu.SMEM((n_rows, KMAX), jnp.int32),
        ],
        compiler_params=pltpu.CompilerParams(vmem_limit_bytes=ATTENTION_VMEM),
        cost_estimate=pl.CostEstimate(flops=ATT_FLOPS, bytes_accessed=0, transcendentals=0),
        name="attention",
    )(coords, block_list, q, *pieces)


def stack_kernel(groups, *refs):
    pieces, outs = refs[: -len(groups)], refs[-len(groups) :]
    for group, out in zip(groups, outs):
        for i, at in enumerate(group):
            out[i] = pieces[at][...]


def stack(pieces, groups):
    return pl.pallas_call(
        functools.partial(stack_kernel, groups),
        out_shape=[
            jax.ShapeDtypeStruct((len(group), *pieces[0].shape), pieces[0].dtype) for group in groups
        ],
        in_specs=[VMEM] * len(pieces),
        out_specs=[VMEM] * len(groups),
        compiler_params=pltpu.CompilerParams(vmem_limit_bytes=PROJECT_VMEM),
        cost_estimate=FREE,
        name="stack",
    )(*pieces)


def project_kernel(steps, coords, own_ref, near_ref, w_ref, w0a, w0b, w1a, w1b, *out_refs):
    core, yl, z = coords[2], coords[3], coords[4]

    def lanes(block):
        return pl.ds(pl.multiple_of(block * 512, 512), 512)

    for step, out_ref in zip(steps, out_refs):
        target = (z + step + NZ) % NZ
        mine = target // 4 == core
        part = lanes(target % 4)
        value = jnp.dot(
            own_ref[...], w_ref[:, lanes(yl * NZ + target)], preferred_element_type=jnp.float32
        )
        value += jnp.dot(
            near_ref[:, :NEAR_ROWS],
            jnp.where(mine, w0a[:, part], w0b[:, part]),
            preferred_element_type=jnp.float32,
        )
        value += jnp.dot(
            near_ref[:, NEAR_ROWS:],
            jnp.where(mine, w1a[:, part], w1b[:, part]),
            preferred_element_type=jnp.float32,
        )
        out_ref[...] = value.astype(jnp.bfloat16)


def project(coords, steps, own, near, weights, parts):
    rows = own.shape[0]
    count = len(steps)
    return pl.pallas_call(
        functools.partial(project_kernel, steps),
        out_shape=[jax.ShapeDtypeStruct((rows, 512), jnp.bfloat16)] * count,
        in_specs=[SMEM] + [VMEM] * 7,
        out_specs=[VMEM] * count,
        compiler_params=pltpu.CompilerParams(vmem_limit_bytes=PROJECT_VMEM),
        cost_estimate=FREE,
        name="project",
    )(coords, own, near, weights, *parts)


def shards(queries, keys_values, block_list, out_weight):
    ctx = lax.axis_index("ctx")
    tp = lax.axis_index("tp")
    coords = jnp.stack([ctx // 4, (ctx // 2) % 2, ctx % 2, tp // NZ, tp % NZ]).astype(jnp.int32)
    n_rows = queries.shape[0] // BLOCK // CHUNKS
    barrier = lax.optimization_barrier

    yl, z = tp // NZ, tp % NZ
    own = lax.dynamic_slice_in_dim(keys_values, (yl * 4 + z // 2) * HD, HD, 2)
    for_far = lax.dynamic_slice_in_dim(keys_values, ((1 - yl) * 4 + z // 2) * HD, HD, 2)
    far = send(for_far, "y_far")
    left = send(own, "x+")
    right = send(own, "x-")

    near_w, far_w = pick(coords, out_weight)
    far, left, right, near_w = barrier((far, left, right, near_w))
    near_part = send(near_w, "y_near")
    one, other = stack([own, far, left, right], ((1, 2), (0, 3)))
    both = send(one, "x+")
    far_right = send(far, "x-")
    one_t = send(one, "core")
    other_t = send(other, "core")
    far_w, _ = barrier((far_w, other_t))
    far_part = send(far_w, "y_far")
    two_far = send(far_right, "x-")
    late = [both, far_right, two_far]
    pieces = [one, other, one_t, other_t, *late, *(send(piece, "core") for piece in late)]
    slots = ((2, 12), (0, 4), (3, 13), (1, 5), (14, 8), (6,), (10,), (15, 9), (7,), (11,))

    attended = [
        attention(coords, block_list, queries, k * n_rows, n_rows, pieces, slots)
        for k in range(CHUNKS)
    ]
    near = [send(done, "y_near") for done in attended]
    near_part, far_part, _ = barrier((near_part, far_part, attended[0]))
    near_other = send(near_part, "core")
    far_part, near_other = barrier((far_part, near_other))
    parts = [near_part, near_other, far_part, send(far_part, "core")]

    def add(*terms):
        return sum(t.astype(jnp.float32) for t in terms).astype(jnp.bfloat16)

    moves = ("z+", "z-")
    ways, moving = [], []
    for k in range(CHUNKS):
        orders = ((4, 3, 2, 1), (-3, -2, -1)) if k % 2 == 0 else ((3, 2, 1), (-4, -3, -2, -1))
        if k:
            near[k], moving[k - 1][1] = barrier((near[k], moving[k - 1][1]))
        early = tuple(order[0] for order in orders)
        late = (*orders[0][1:], *orders[1][1:], 0)
        begun = project(coords, early, attended[k], near[k], out_weight, parts)
        moving.append([send(value, move) for value, move in zip(begun, moves)])
        partial = dict(zip(late, project(coords, late, attended[k], near[k], out_weight, parts)))
        ways.append((orders, partial))

    for step in range(1, 4):
        for k in range(CHUNKS):
            orders, partial = ways[k]
            for way, order in enumerate(orders):
                if step < len(order):
                    moving[k][way] = send(add(moving[k][way], partial[order[step]]), moves[way])
    results = [add(ways[k][1][0], *moving[k]) for k in range(CHUNKS)]
    return jnp.concatenate(results, 0)


def solution(mesh):
    in_specs = (P("ctx", "tp"), P(None, "ctx", None), P("ctx", None), P("tp", None))
    return jax.shard_map(
        shards, mesh=mesh, in_specs=in_specs, out_specs=P("ctx", "tp"), check_vma=False
    )
```

```python
import functools
import math

import jax
import jax.numpy as jnp
from jax import lax
from jax.experimental import pallas as pl
from jax.experimental.pallas import tpu as pltpu
from jax.sharding import PartitionSpec as P

HD = 128
BLOCK = 128
KMAX = 16
GROUP = 4
AXES = ("ctx", "tp")
NX, NYH, NC, NYL, NZ = 4, 2, 2, 2, 8
SLOTS = NX * NYH * NC
SCALE2 = HD ** (-0.5) * math.log2(math.e)
CHUNKS = 2
LOW = -1e30
NEAR_ROWS = 256
ATTENTION_VMEM = 14 * 2**20
PROJECT_VMEM = 8 * 2**20
WIDE = 4
MARK_FLOPS = 0
ATT_FLOPS = 0
VMEM_LIMIT = 50 * 2**20
FREE = pl.CostEstimate(flops=0, bytes_accessed=0, transcendentals=0)


def pairs(move):
    out = []
    for x in range(NX):
        for y in range(4):
            for c in range(NC):
                for z in range(NZ):
                    x2, y2, c2, z2 = move(x, y, c, z)
                    x2, y2, c2, z2 = x2 % NX, y2 % 4, c2 % NC, z2 % NZ

                    def index(x, y, c, z):
                        return (x * 4 + (y // 2) * 2 + c) * 16 + (y % 2) * 8 + z

                    out.append((index(x, y, c, z), index(x2, y2, c2, z2)))
    return out


MOVES = {
    "x+": pairs(lambda x, y, c, z: (x + 1, y, c, z)),
    "x-": pairs(lambda x, y, c, z: (x - 1, y, c, z)),
    "z+": pairs(lambda x, y, c, z: (x, y, c, z + 1)),
    "z-": pairs(lambda x, y, c, z: (x, y, c, z - 1)),
    "core": pairs(lambda x, y, c, z: (x, y, c + 1, z)),
    "y_near": pairs(lambda x, y, c, z: (x, y ^ 1, c, z)),
    "y_far": pairs(lambda x, y, c, z: (x, 3 - y, c, z)),
}


def send(array, move):
    return lax.ppermute(array, AXES, MOVES[move])


SMEM = pl.BlockSpec(memory_space=pltpu.SMEM)
VMEM = pl.BlockSpec(memory_space=pltpu.VMEM)
HBM = pl.BlockSpec(memory_space=pltpu.HBM)


def pick_kernel(coords, w_ref, near_w_ref, far_w_ref, sems):
    c, yl = coords[2], coords[3]
    columns = near_w_ref.shape[1]
    near_rows, far_rows = near_w_ref.shape[0], far_w_ref.shape[0]
    there = pl.ds(pl.multiple_of(((1 - yl) * 2 + c) * columns, columns), columns)
    copies = [
        pltpu.make_async_copy(w_ref.at[pl.ds(0, near_rows), there], near_w_ref, sems.at[0]),
        pltpu.make_async_copy(w_ref.at[pl.ds(near_rows, far_rows), there], far_w_ref, sems.at[1]),
    ]
    for copy in copies:
        copy.start()
    for copy in copies:
        copy.wait()


def pick(coords, weights):
    depth, full = weights.shape
    parts = [jax.ShapeDtypeStruct((n, full // 4), jnp.bfloat16) for n in (NEAR_ROWS, depth - NEAR_ROWS)]
    return pl.pallas_call(
        pick_kernel,
        out_shape=parts,
        in_specs=[SMEM, HBM],
        out_specs=[VMEM] * 2,
        scratch_shapes=[pltpu.SemaphoreType.DMA((2,))],
        compiler_params=pltpu.CompilerParams(vmem_limit_bytes=VMEM_LIMIT),
        cost_estimate=FREE,
        name="pick",
    )(coords, weights)


def attention_kernel(first_row, n_rows, slots, coords, block_list, q_ref, *refs):
    if slots:
        pieces, refs = refs[: len(slots)], refs[len(slots) :]
        out_ref, kv, scores, top, total, acc, placed = refs
        for piece, held in zip(pieces, slots):
            for i, slot in enumerate(held):
                kv[:, slot * 512 : (slot + 1) * 512, :] = piece[i] if len(held) > 1 else piece[...]
    else:
        kv, refs = refs[0], refs[1:]
        before, refs = refs[:-6], refs[-6:]
        out_ref, scores, top, total, acc, placed = refs
        done = 0
        for ref in before:
            out_ref[done : done + ref.shape[0], :] = ref[...]
            done += ref.shape[0]
    ahead = out_ref.shape[0] - n_rows * BLOCK
    x, yh, c = coords[0], coords[1], coords[2]

    counts = []
    for row in range(n_rows):

        def place(j, count):
            block = block_list[first_row + row, j]
            shard = jnp.maximum(block, 0) // 4
            slot = ((shard // 4 - x) % NX) * 4 + (((shard // 2) % 2 - yh) % 2) * 2 + (shard - c) % 2
            placed[row, j] = (slot * 4 + block % 4) * BLOCK
            return count + (block >= 0).astype(jnp.int32)

        counts.append(lax.fori_loop(0, KMAX, place, 0))

    for row in range(n_rows):
        count = counts[row]
        groups = (count + WIDE - 1) // WIDE

        def gather(which, group):
            tiles = []
            for i in range(WIDE):
                j = jnp.minimum(group * WIDE + i, count - 1)
                tiles.append(kv[which, pl.ds(pl.multiple_of(placed[row, j], BLOCK), BLOCK), :])
            return jnp.concatenate(tiles, 0)

        rows = slice((first_row + row) * BLOCK, (first_row + row + 1) * BLOCK)
        q = jnp.concatenate([q_ref[rows, g * HD : (g + 1) * HD] for g in range(GROUP)], 0)
        top[...] = jnp.full(top.shape, LOW, jnp.float32)

        def first(group, carry):
            s = lax.dot_general(
                q, gather(0, group), (((1,), (1,)), ((), ())), preferred_element_type=jnp.float32
            )
            high = top[...]
            for i in range(WIDE):
                tile = s[:, i * BLOCK : (i + 1) * BLOCK]
                if i:
                    tile = jnp.where(group * WIDE + i < count, tile, LOW)
                scores[group, :, i * BLOCK : (i + 1) * BLOCK] = tile
                high = jnp.maximum(high, tile)
            top[...] = high
            return carry

        lax.fori_loop(0, groups, first, 0)
        top[...] = jnp.broadcast_to(jnp.max(top[...], axis=1, keepdims=True) * SCALE2, top.shape)
        total[...] = jnp.zeros(total.shape, jnp.float32)
        acc[...] = jnp.zeros(acc.shape, jnp.float32)

        def second(group, carry):
            high = top[...]
            added, weights = total[...], []
            for i in range(WIDE):
                tile = jnp.exp2(scores[group, :, i * BLOCK : (i + 1) * BLOCK] * SCALE2 - high)
                added += tile
                weights.append(tile.astype(jnp.bfloat16))
            total[...] = added
            acc[...] += jnp.dot(
                jnp.concatenate(weights, 1), gather(1, group), preferred_element_type=jnp.float32
            )
            return carry

        lax.fori_loop(0, groups, second, 0)
        result = (acc[...] / jnp.sum(total[...], axis=1, keepdims=True)).astype(jnp.bfloat16)
        here = slice(ahead + row * BLOCK, ahead + (row + 1) * BLOCK)
        for g in range(GROUP):
            out_ref[here, g * HD : (g + 1) * HD] = result[g * BLOCK : (g + 1) * BLOCK, :]


def attention(coords, block_list, q, first_row, n_rows, pieces, slots=()):
    rows = GROUP * BLOCK
    width = q.shape[1]
    tok = n_rows * BLOCK + (0 if slots else sum(piece.shape[0] for piece in pieces[1:]))
    kv_shape = (2, SLOTS * 512, HD)
    out_shape = [jax.ShapeDtypeStruct((tok, width), jnp.bfloat16)]
    if slots:
        out_shape.append(jax.ShapeDtypeStruct(kv_shape, jnp.bfloat16))
    return pl.pallas_call(
        functools.partial(attention_kernel, first_row, n_rows, slots),
        out_shape=out_shape,
        in_specs=[SMEM, SMEM, VMEM] + [VMEM] * len(pieces),
        out_specs=[VMEM] * len(out_shape),
        scratch_shapes=[
            pltpu.VMEM((KMAX // WIDE, rows, WIDE * BLOCK), jnp.float32),
            pltpu.VMEM((rows, HD), jnp.float32),
            pltpu.VMEM((rows, HD), jnp.float32),
            pltpu.VMEM((rows, HD), jnp.float32),
            pltpu.SMEM((n_rows, KMAX), jnp.int32),
        ],
        compiler_params=pltpu.CompilerParams(vmem_limit_bytes=ATTENTION_VMEM),
        cost_estimate=pl.CostEstimate(flops=ATT_FLOPS, bytes_accessed=0, transcendentals=0),
        name="attention",
    )(coords, block_list, q, *pieces)


def stack_kernel(groups, *refs):
    pieces, outs = refs[: -len(groups)], refs[-len(groups) :]
    for group, out in zip(groups, outs):
        at = 0
        for piece in (pieces[i] for i in group):
            n = piece.shape[0] if len(piece.shape) == 4 else 1
            out[at : at + n] = piece[...].reshape(n, *out.shape[1:])
            at += n


def stack(pieces, groups):
    sizes = [piece.shape[0] if piece.ndim == 4 else 1 for piece in pieces]
    shape, dtype = pieces[0].shape[-3:], pieces[0].dtype
    return pl.pallas_call(
        functools.partial(stack_kernel, groups),
        out_shape=[
            jax.ShapeDtypeStruct((sum(sizes[i] for i in group), *shape), dtype) for group in groups
        ],
        in_specs=[VMEM] * len(pieces),
        out_specs=[VMEM] * len(groups),
        compiler_params=pltpu.CompilerParams(vmem_limit_bytes=PROJECT_VMEM),
        cost_estimate=FREE,
        name="stack",
    )(*pieces)


def mark_kernel(coords, *refs):
    for i in range(coords.shape[0]):
        refs[-1][i] = coords[i]


def mark(coords, *arrays):
    return pl.pallas_call(
        mark_kernel,
        out_shape=jax.ShapeDtypeStruct(coords.shape, coords.dtype),
        in_specs=[SMEM] + [VMEM] * len(arrays),
        out_specs=SMEM,
        compiler_params=pltpu.CompilerParams(vmem_limit_bytes=PROJECT_VMEM),
        cost_estimate=pl.CostEstimate(flops=MARK_FLOPS, bytes_accessed=0, transcendentals=0),
        name="mark",
    )(coords, *arrays)


def project_kernel(steps, coords, own_ref, near_ref, w_ref, w0a, w0b, w1a, w1b, *out_refs):
    core, yl, z = coords[2], coords[3], coords[4]

    def lanes(block):
        return pl.ds(pl.multiple_of(block * 512, 512), 512)

    for step, out_ref in zip(steps, out_refs):
        target = (z + step + NZ) % NZ
        mine = target // 4 == core
        part = lanes(target % 4)
        value = jnp.dot(
            own_ref[...], w_ref[:, lanes(yl * NZ + target)], preferred_element_type=jnp.float32
        )
        value += jnp.dot(
            near_ref[:, :NEAR_ROWS],
            jnp.where(mine, w0a[:, part], w0b[:, part]),
            preferred_element_type=jnp.float32,
        )
        value += jnp.dot(
            near_ref[:, NEAR_ROWS:],
            jnp.where(mine, w1a[:, part], w1b[:, part]),
            preferred_element_type=jnp.float32,
        )
        out_ref[...] = value.astype(jnp.bfloat16)


def project(coords, steps, own, near, weights, parts):
    rows = own.shape[0]
    count = len(steps)
    return pl.pallas_call(
        functools.partial(project_kernel, steps),
        out_shape=[jax.ShapeDtypeStruct((rows, 512), jnp.bfloat16)] * count,
        in_specs=[SMEM] + [VMEM] * 7,
        out_specs=[VMEM] * count,
        compiler_params=pltpu.CompilerParams(vmem_limit_bytes=PROJECT_VMEM),
        cost_estimate=FREE,
        name="project",
    )(coords, own, near, weights, *parts)


def shards(queries, keys_values, block_list, out_weight):
    ctx = lax.axis_index("ctx")
    tp = lax.axis_index("tp")
    coords = jnp.stack([ctx // 4, (ctx // 2) % 2, ctx % 2, tp // NZ, tp % NZ]).astype(jnp.int32)
    n_rows = queries.shape[0] // BLOCK // CHUNKS
    barrier = lax.optimization_barrier

    yl, z = tp // NZ, tp % NZ
    own = lax.dynamic_slice_in_dim(keys_values, (yl * 4 + z // 2) * HD, HD, 2)
    for_far = lax.dynamic_slice_in_dim(keys_values, ((1 - yl) * 4 + z // 2) * HD, HD, 2)
    far = send(for_far, "y_far")
    left = send(own, "x+")
    right = send(own, "x-")

    near_w, far_w = pick(coords, out_weight)
    far, left, right, near_w, far_w = barrier((far, left, right, near_w, far_w))
    near_part = send(near_w, "y_near")
    far_part = send(far_w, "y_far")
    one, four = stack([own, far, left, right], ((1, 2), (0, 1, 2, 3)))
    far_right = send(far, "x-")
    both = send(one, "x+")
    two_far = send(far_right, "x-")
    late = [both, far_right, two_far]
    pieces = [four, send(four, "core"), *late, *(send(piece, "core") for piece in late)]
    slots = ((0, 2, 12, 4), (1, 3, 13, 5), (14, 8), (6,), (10,), (15, 9), (7,), (11,))

    first, kv = attention(coords, block_list, queries, 0, n_rows, pieces, slots)
    attended = [first] + [
        attention(coords, block_list, queries, k * n_rows, n_rows, [kv])[0] for k in range(1, CHUNKS)
    ]
    near = [send(first, "y_near"), None]
    near_part, far_part, near[0], near[1] = barrier((near_part, far_part, near[0], attended[1]))
    near[1] = send(near[1], "y_near")
    near_other, far_other = send(near_part, "core"), send(far_part, "core")
    parts = [near_part, near_other, far_part, far_other]
    coords = mark(coords, near_other, far_other)

    def add(*terms):
        return sum(t.astype(jnp.float32) for t in terms).astype(jnp.bfloat16)

    moves = ("z+", "z-")
    ways, moving = [], []
    for k in range(CHUNKS):
        orders = ((4, 3, 2, 1), (-3, -2, -1)) if k % 2 == 0 else ((3, 2, 1), (-4, -3, -2, -1))
        if k:
            near[k], moving[k - 1][1] = barrier((near[k], moving[k - 1][1]))
        early = tuple(order[0] for order in orders)
        late = (*orders[0][1:], *orders[1][1:], 0)
        begun = project(coords, early, attended[k], near[k], out_weight, parts)
        moving.append([send(value, move) for value, move in zip(begun, moves)])
        partial = dict(zip(late, project(coords, late, attended[k], near[k], out_weight, parts)))
        ways.append((orders, partial))

    for step in range(1, 4):
        for k in range(CHUNKS):
            orders, partial = ways[k]
            for way, order in enumerate(orders):
                if step < len(order):
                    moving[k][way] = send(add(moving[k][way], partial[order[step]]), moves[way])
    results = [add(ways[k][1][0], *moving[k]) for k in range(CHUNKS)]
    return jnp.concatenate(results, 0)


def solution(mesh):
    in_specs = (P("ctx", "tp"), P(None, "ctx", None), P("ctx", None), P("tp", None))
    return jax.shard_map(
        shards, mesh=mesh, in_specs=in_specs, out_specs=P("ctx", "tp"), check_vma=False
    )
```

```python
import functools
import math

import jax
import jax.numpy as jnp
from jax import lax
from jax.experimental import pallas as pl
from jax.experimental.pallas import tpu as pltpu
from jax.sharding import PartitionSpec as P

HD = 128
BLOCK = 128
KMAX = 16
GROUP = 4
AXES = ("ctx", "tp")
NX, NYH, NC, NYL, NZ = 4, 2, 2, 2, 8
SLOTS = NX * NYH * NC
SCALE2 = HD ** (-0.5) * math.log2(math.e)
CHUNKS = 2
LOW = -1e30
NEAR_ROWS = 256
ATTENTION_VMEM = 14 * 2**20
PROJECT_VMEM = 8 * 2**20
WIDE = 4
ATT_FLOPS = 0
VMEM_LIMIT = 50 * 2**20
FREE = pl.CostEstimate(flops=0, bytes_accessed=0, transcendentals=0)


def pairs(move, sends=lambda x, y, c, z: True):
    out = []
    for x in range(NX):
        for y in range(4):
            for c in range(NC):
                for z in range(NZ):
                    x2, y2, c2, z2 = move(x, y, c, z)
                    x2, y2, c2, z2 = x2 % NX, y2 % 4, c2 % NC, z2 % NZ

                    def index(x, y, c, z):
                        return (x * 4 + (y // 2) * 2 + c) * 16 + (y % 2) * 8 + z

                    if sends(x, y, c, z):
                        out.append((index(x, y, c, z), index(x2, y2, c2, z2)))
    return out


MOVES = {
    "x+": pairs(lambda x, y, c, z: (x + 1, y, c, z)),
    "x-": pairs(lambda x, y, c, z: (x - 1, y, c, z)),
    "z+": pairs(lambda x, y, c, z: (x, y, c, z + 1)),
    "z-": pairs(lambda x, y, c, z: (x, y, c, z - 1)),
    **{
        f"swing{sign}{parity}": pairs(
            lambda x, y, c, z: (x, y, c, z + (sign if (z + c) % 2 == parity else -sign))
        )
        for sign in (1, -1)
        for parity in (0, 1)
    },
    **{
        f"last{sign}": pairs(
            lambda x, y, c, z: (x, y, c, z + sign), lambda x, y, c, z: (z + c) % 2 == 1
        )
        for sign in (1, -1)
    },
    "core": pairs(lambda x, y, c, z: (x, y, c + 1, z)),
    "y_near": pairs(lambda x, y, c, z: (x, y ^ 1, c, z)),
    "y_far": pairs(lambda x, y, c, z: (x, 3 - y, c, z)),
}


def send(array, move):
    return lax.ppermute(array, AXES, MOVES[move])


SMEM = pl.BlockSpec(memory_space=pltpu.SMEM)
VMEM = pl.BlockSpec(memory_space=pltpu.VMEM)
HBM = pl.BlockSpec(memory_space=pltpu.HBM)


REACH = ((4, -2, 2, 0), (-3, 3, -1, 1))


def pick_kernel(coords, w_ref, near_w_ref, far_w_ref, sems):
    c, yl = coords[2], coords[3]
    copies = []
    for j in range(NZ // 2):
        there = pl.ds(pl.multiple_of(((1 - yl) * NZ + 2 * j + c) * 512, 512), 512)
        here = pl.ds(j * 512, 512)
        row = 0
        for i, out in enumerate((near_w_ref, far_w_ref)):
            rows = pl.ds(row, out.shape[0])
            copies.append(
                pltpu.make_async_copy(w_ref.at[rows, there], out.at[:, here], sems.at[2 * j + i])
            )
            row += out.shape[0]
    for copy in copies:
        copy.start()
    for copy in copies:
        copy.wait()


def pick(coords, weights):
    depth, full = weights.shape
    parts = [jax.ShapeDtypeStruct((n, full // 4), jnp.bfloat16) for n in (NEAR_ROWS, depth - NEAR_ROWS)]
    return pl.pallas_call(
        pick_kernel,
        out_shape=parts,
        in_specs=[SMEM, HBM],
        out_specs=[VMEM] * 2,
        scratch_shapes=[pltpu.SemaphoreType.DMA((NZ,))],
        compiler_params=pltpu.CompilerParams(vmem_limit_bytes=VMEM_LIMIT),
        cost_estimate=FREE,
        name="pick",
    )(coords, weights)


def attention_kernel(first_row, n_rows, slots, coords, block_list, q_ref, *refs):
    if slots:
        pieces, refs = refs[: len(slots)], refs[len(slots) :]
        out_ref, kv, scores, top, total, acc, placed = refs
        for piece, held in zip(pieces, slots):
            for i, slot in enumerate(held):
                kv[:, slot * 512 : (slot + 1) * 512, :] = piece[i] if len(held) > 1 else piece[...]
    else:
        kv, refs = refs[0], refs[1:]
        before, refs = refs[:-6], refs[-6:]
        out_ref, scores, top, total, acc, placed = refs
        done = 0
        for ref in before:
            out_ref[done : done + ref.shape[0], :] = ref[...]
            done += ref.shape[0]
    ahead = out_ref.shape[0] - n_rows * BLOCK
    x, yh, c = coords[0], coords[1], coords[2]

    counts = []
    for row in range(n_rows):

        def place(j, count):
            block = block_list[first_row + row, j]
            shard = jnp.maximum(block, 0) // 4
            slot = ((shard // 4 - x) % NX) * 4 + (((shard // 2) % 2 - yh) % 2) * 2 + (shard - c) % 2
            placed[row, j] = (slot * 4 + block % 4) * BLOCK
            return count + (block >= 0).astype(jnp.int32)

        counts.append(lax.fori_loop(0, KMAX, place, 0))

    for row in range(n_rows):
        count = counts[row]
        groups = (count + WIDE - 1) // WIDE

        def gather(which, group):
            tiles = []
            for i in range(WIDE):
                j = jnp.minimum(group * WIDE + i, count - 1)
                tiles.append(kv[which, pl.ds(pl.multiple_of(placed[row, j], BLOCK), BLOCK), :])
            return jnp.concatenate(tiles, 0)

        rows = slice((first_row + row) * BLOCK, (first_row + row + 1) * BLOCK)
        q = jnp.concatenate([q_ref[rows, g * HD : (g + 1) * HD] for g in range(GROUP)], 0)
        top[...] = jnp.full(top.shape, LOW, jnp.float32)

        def first(group, carry):
            s = lax.dot_general(
                q, gather(0, group), (((1,), (1,)), ((), ())), preferred_element_type=jnp.float32
            )
            high = top[...]
            for i in range(WIDE):
                tile = s[:, i * BLOCK : (i + 1) * BLOCK]
                if i:
                    tile = jnp.where(group * WIDE + i < count, tile, LOW)
                scores[group, :, i * BLOCK : (i + 1) * BLOCK] = tile
                high = jnp.maximum(high, tile)
            top[...] = high
            return carry

        lax.fori_loop(0, groups, first, 0)
        top[...] = jnp.broadcast_to(jnp.max(top[...], axis=1, keepdims=True) * SCALE2, top.shape)
        total[...] = jnp.zeros(total.shape, jnp.float32)
        acc[...] = jnp.zeros(acc.shape, jnp.float32)

        def second(group, carry):
            high = top[...]
            added, weights = total[...], []
            for i in range(WIDE):
                tile = jnp.exp2(scores[group, :, i * BLOCK : (i + 1) * BLOCK] * SCALE2 - high)
                added += tile
                weights.append(tile.astype(jnp.bfloat16))
            total[...] = added
            acc[...] += jnp.dot(
                jnp.concatenate(weights, 1), gather(1, group), preferred_element_type=jnp.float32
            )
            return carry

        lax.fori_loop(0, groups, second, 0)
        result = (acc[...] / jnp.sum(total[...], axis=1, keepdims=True)).astype(jnp.bfloat16)
        here = slice(ahead + row * BLOCK, ahead + (row + 1) * BLOCK)
        for g in range(GROUP):
            out_ref[here, g * HD : (g + 1) * HD] = result[g * BLOCK : (g + 1) * BLOCK, :]


def attention(coords, block_list, q, first_row, n_rows, pieces, slots=()):
    rows = GROUP * BLOCK
    width = q.shape[1]
    tok = n_rows * BLOCK + (0 if slots else sum(piece.shape[0] for piece in pieces[1:]))
    kv_shape = (2, SLOTS * 512, HD)
    out_shape = [jax.ShapeDtypeStruct((tok, width), jnp.bfloat16)]
    if slots:
        out_shape.append(jax.ShapeDtypeStruct(kv_shape, jnp.bfloat16))
    return pl.pallas_call(
        functools.partial(attention_kernel, first_row, n_rows, slots),
        out_shape=out_shape,
        in_specs=[SMEM, SMEM, VMEM] + [VMEM] * len(pieces),
        out_specs=[VMEM] * len(out_shape),
        scratch_shapes=[
            pltpu.VMEM((KMAX // WIDE, rows, WIDE * BLOCK), jnp.float32),
            pltpu.VMEM((rows, HD), jnp.float32),
            pltpu.VMEM((rows, HD), jnp.float32),
            pltpu.VMEM((rows, HD), jnp.float32),
            pltpu.SMEM((n_rows, KMAX), jnp.int32),
        ],
        compiler_params=pltpu.CompilerParams(vmem_limit_bytes=ATTENTION_VMEM),
        cost_estimate=pl.CostEstimate(flops=ATT_FLOPS, bytes_accessed=0, transcendentals=0),
        name="attention",
    )(coords, block_list, q, *pieces)


def stack_kernel(groups, *refs):
    pieces, outs = refs[: -len(groups)], refs[-len(groups) :]
    for group, out in zip(groups, outs):
        at = 0
        for piece in (pieces[i] for i in group):
            n = piece.shape[0] if len(piece.shape) == 4 else 1
            out[at : at + n] = piece[...].reshape(n, *out.shape[1:])
            at += n


def stack(pieces, groups):
    sizes = [piece.shape[0] if piece.ndim == 4 else 1 for piece in pieces]
    shape, dtype = pieces[0].shape[-3:], pieces[0].dtype
    return pl.pallas_call(
        functools.partial(stack_kernel, groups),
        out_shape=[
            jax.ShapeDtypeStruct((sum(sizes[i] for i in group), *shape), dtype) for group in groups
        ],
        in_specs=[VMEM] * len(pieces),
        out_specs=[VMEM] * len(groups),
        compiler_params=pltpu.CompilerParams(vmem_limit_bytes=PROJECT_VMEM),
        cost_estimate=FREE,
        name="stack",
    )(*pieces)


def project_kernel(
    steps, sign, coords, own_ref, other_ref, near_ref, other_near_ref, w_ref, w0_ref, w1_ref, *out_refs
):
    c, yl, z = coords[2], coords[3], coords[4]
    odd = (z + c) % 2
    own = jnp.concatenate([own_ref[...], other_ref[...]], 0)
    near = jnp.concatenate([near_ref[...], other_near_ref[...]], 0)

    def lanes(block):
        return pl.ds(pl.multiple_of(block * 512, 512), 512)

    for step, out_ref in zip(steps, out_refs):
        target = (z + sign * jnp.where(odd == 0, REACH[0][step], REACH[1][step]) + NZ) % NZ
        part = lanes(target // 2)
        value = jnp.dot(
            own, w_ref[:, lanes(yl * NZ + target)], preferred_element_type=jnp.float32
        )
        value += jnp.dot(near[:, :NEAR_ROWS], w0_ref[:, part], preferred_element_type=jnp.float32)
        value += jnp.dot(near[:, NEAR_ROWS:], w1_ref[:, part], preferred_element_type=jnp.float32)
        out_ref[...] = value.astype(jnp.bfloat16)


def project(coords, steps, sign, rows, weights, parts):
    count = len(steps)
    shape = (2 * rows[0].shape[0], 512)
    return pl.pallas_call(
        functools.partial(project_kernel, steps, sign),
        out_shape=[jax.ShapeDtypeStruct(shape, jnp.bfloat16)] * count,
        in_specs=[SMEM] + [VMEM] * 7,
        out_specs=[VMEM] * count,
        compiler_params=pltpu.CompilerParams(vmem_limit_bytes=PROJECT_VMEM),
        cost_estimate=FREE,
        name="project",
    )(coords, *rows, weights, *parts)


def shards(queries, keys_values, block_list, out_weight):
    ctx = lax.axis_index("ctx")
    tp = lax.axis_index("tp")
    coords = jnp.stack([ctx // 4, (ctx // 2) % 2, ctx % 2, tp // NZ, tp % NZ]).astype(jnp.int32)
    n_rows = queries.shape[0] // BLOCK // CHUNKS
    barrier = lax.optimization_barrier

    yl, z = tp // NZ, tp % NZ
    own = lax.dynamic_slice_in_dim(keys_values, (yl * 4 + z // 2) * HD, HD, 2)
    for_far = lax.dynamic_slice_in_dim(keys_values, ((1 - yl) * 4 + z // 2) * HD, HD, 2)
    far = send(for_far, "y_far")
    left = send(own, "x+")
    right = send(own, "x-")

    near_w, far_w = pick(coords, out_weight)
    near_part = send(near_w, "y_near")
    far_part = send(far_w, "y_far")

    one, four = stack([own, far, left, right], ((1, 2), (0, 1, 2, 3)))

    def spread(_, held):
        far, one, four, _ = held
        far_right = send(far, "x-")
        both = send(one, "x+")
        return (far_right, both, send(four, "core"), send(far_right, "x-"))

    once = (ctx >= 0).astype(jnp.int32)
    far_right, both, four_t, two_far = lax.fori_loop(0, once, spread, (far, one, four, right))
    late = [both, far_right, two_far]
    pieces = [four, four_t, *late, *(send(piece, "core") for piece in late)]
    slots = ((0, 2, 12, 4), (1, 3, 13, 5), (14, 8), (6,), (10,), (15, 9), (7,), (11,))

    first, kv = attention(coords, block_list, queries, 0, n_rows, pieces, slots)
    kv, near_part, far_part = barrier((kv, near_part, far_part))
    parts = [near_part, far_part]
    second = attention(coords, block_list, queries, n_rows, n_rows, [kv])[0]
    near = send(first, "y_near")
    near, second = barrier((near, second))
    rows = [
        (a, send(a, "core"), n, send(n, "core"))
        for a, n in ((first, near), (second, send(second, "y_near")))
    ]

    def add(a, b):
        return (a.astype(jnp.float32) + b.astype(jnp.float32)).astype(jnp.bfloat16)

    signs = (1, -1)
    moving, partial = [], []
    for k in range(CHUNKS):
        if k:
            tied = barrier((*rows[k], moving[k - 1]))
            rows[k], moving[k - 1] = tied[:-1], tied[-1]
        (begun,) = project(coords, (0,), signs[k], rows[k], out_weight, parts)
        moving.append(send(begun, f"swing{signs[k]}0"))
        partial.append(list(project(coords, (1, 2, 3), signs[k], rows[k], out_weight, parts)))
    for step in range(1, 4):
        for k in range(CHUNKS):
            partial[k][step - 1] = add(moving[k], partial[k][step - 1])
            move = f"swing{signs[k]}{step % 2}" if step < 3 else f"last{signs[k]}"
            moving[k] = send(partial[k][step - 1], move)
    results = []
    for k in range(CHUNKS):
        whole = add(partial[k][2], moving[k])
        half = whole.shape[0] // 2
        other = send(whole[half:], "core")
        results.append(jnp.where((ctx + z) % 2 == 0, whole[:half], other))
    return jnp.concatenate(results, 0)


def solution(mesh):
    in_specs = (P("ctx", "tp"), P(None, "ctx", None), P("ctx", None), P("tp", None))
    return jax.shard_map(
        shards, mesh=mesh, in_specs=in_specs, out_specs=P("ctx", "tp"), check_vma=False
    )
```

```python
import functools
import math

import jax
import jax.numpy as jnp
from jax import lax
from jax.experimental import pallas as pl
from jax.experimental.pallas import tpu as pltpu
from jax.sharding import PartitionSpec as P

HD = 128
BLOCK = 128
KMAX = 16
GROUP = 4
AXES = ("ctx", "tp")
NX, NYH, NC, NYL, NZ = 4, 2, 2, 2, 8
SLOTS = NX * NYH * NC
SCALE2 = HD ** (-0.5) * math.log2(math.e)
CHUNKS = 2
LOW = -1e30
NEAR_ROWS = 224
ATTENTION_VMEM = 14 * 2**20
PROJECT_VMEM = 8 * 2**20
WIDE = 4
ATT_FLOPS = 0
VMEM_LIMIT = 50 * 2**20
FREE = pl.CostEstimate(flops=0, bytes_accessed=0, transcendentals=0)


def pairs(move):
    out = []
    for x in range(NX):
        for y in range(4):
            for c in range(NC):
                for z in range(NZ):
                    x2, y2, c2, z2 = move(x, y, c, z)
                    x2, y2, c2, z2 = x2 % NX, y2 % 4, c2 % NC, z2 % NZ

                    def index(x, y, c, z):
                        return (x * 4 + (y // 2) * 2 + c) * 16 + (y % 2) * 8 + z

                    out.append((index(x, y, c, z), index(x2, y2, c2, z2)))
    return out


MOVES = {
    "x+": pairs(lambda x, y, c, z: (x + 1, y, c, z)),
    "x-": pairs(lambda x, y, c, z: (x - 1, y, c, z)),
    "z+": pairs(lambda x, y, c, z: (x, y, c, z + 1)),
    "z-": pairs(lambda x, y, c, z: (x, y, c, z - 1)),
    "core": pairs(lambda x, y, c, z: (x, y, c + 1, z)),
    "y_near": pairs(lambda x, y, c, z: (x, y ^ 1, c, z)),
    "y_far": pairs(lambda x, y, c, z: (x, 3 - y, c, z)),
}


def send(array, move):
    return lax.ppermute(array, AXES, MOVES[move])


SMEM = pl.BlockSpec(memory_space=pltpu.SMEM)
VMEM = pl.BlockSpec(memory_space=pltpu.VMEM)
HBM = pl.BlockSpec(memory_space=pltpu.HBM)


def pick_kernel(coords, w_ref, near_w_ref, far_w_ref, sems):
    c, yl = coords[2], coords[3]
    columns = near_w_ref.shape[1]
    near_rows, far_rows = near_w_ref.shape[0], far_w_ref.shape[0]
    there = pl.ds(pl.multiple_of(((1 - yl) * 2 + c) * columns, columns), columns)
    copies = [
        pltpu.make_async_copy(w_ref.at[pl.ds(0, near_rows), there], near_w_ref, sems.at[0]),
        pltpu.make_async_copy(w_ref.at[pl.ds(near_rows, far_rows), there], far_w_ref, sems.at[1]),
    ]
    for copy in copies:
        copy.start()
    for copy in copies:
        copy.wait()


def pick(coords, weights):
    depth, full = weights.shape
    parts = [jax.ShapeDtypeStruct((n, full // 4), jnp.bfloat16) for n in (NEAR_ROWS, depth - NEAR_ROWS)]
    return pl.pallas_call(
        pick_kernel,
        out_shape=parts,
        in_specs=[SMEM, HBM],
        out_specs=[VMEM] * 2,
        scratch_shapes=[pltpu.SemaphoreType.DMA((2,))],
        compiler_params=pltpu.CompilerParams(vmem_limit_bytes=VMEM_LIMIT),
        cost_estimate=FREE,
        name="pick",
    )(coords, weights)


def attention_kernel(first_row, n_rows, slots, coords, block_list, q_ref, *refs):
    if slots:
        pieces, refs = refs[: len(slots)], refs[len(slots) :]
        out_ref, kv, scores, top, total, acc, placed = refs
        for piece, held in zip(pieces, slots):
            for i, slot in enumerate(held):
                kv[:, slot * 512 : (slot + 1) * 512, :] = piece[i] if len(held) > 1 else piece[...]
    else:
        kv, refs = refs[0], refs[1:]
        before, refs = refs[:-6], refs[-6:]
        out_ref, scores, top, total, acc, placed = refs
        done = 0
        for ref in before:
            out_ref[done : done + ref.shape[0], :] = ref[...]
            done += ref.shape[0]
    ahead = out_ref.shape[0] - n_rows * BLOCK
    x, yh, c = coords[0], coords[1], coords[2]

    counts = []
    for row in range(n_rows):

        def place(j, count):
            block = block_list[first_row + row, j]
            shard = jnp.maximum(block, 0) // 4
            slot = ((shard // 4 - x) % NX) * 4 + (((shard // 2) % 2 - yh) % 2) * 2 + (shard - c) % 2
            placed[row, j] = (slot * 4 + block % 4) * BLOCK
            return count + (block >= 0).astype(jnp.int32)

        counts.append(lax.fori_loop(0, KMAX, place, 0))

    for row in range(n_rows):
        count = counts[row]
        groups = (count + WIDE - 1) // WIDE

        def gather(which, group):
            tiles = []
            for i in range(WIDE):
                j = jnp.minimum(group * WIDE + i, count - 1)
                tiles.append(kv[which, pl.ds(pl.multiple_of(placed[row, j], BLOCK), BLOCK), :])
            return jnp.concatenate(tiles, 0)

        rows = slice((first_row + row) * BLOCK, (first_row + row + 1) * BLOCK)
        q = jnp.concatenate([q_ref[rows, g * HD : (g + 1) * HD] for g in range(GROUP)], 0)
        top[...] = jnp.full(top.shape, LOW, jnp.float32)

        def first(group, carry):
            s = lax.dot_general(
                q, gather(0, group), (((1,), (1,)), ((), ())), preferred_element_type=jnp.float32
            )
            high = top[...]
            for i in range(WIDE):
                tile = s[:, i * BLOCK : (i + 1) * BLOCK]
                if i:
                    tile = jnp.where(group * WIDE + i < count, tile, LOW)
                scores[group, :, i * BLOCK : (i + 1) * BLOCK] = tile
                high = jnp.maximum(high, tile)
            top[...] = high
            return carry

        lax.fori_loop(0, groups, first, 0)
        top[...] = jnp.broadcast_to(jnp.max(top[...], axis=1, keepdims=True) * SCALE2, top.shape)
        total[...] = jnp.zeros(total.shape, jnp.float32)
        acc[...] = jnp.zeros(acc.shape, jnp.float32)

        def second(group, carry):
            high = top[...]
            added, weights = total[...], []
            for i in range(WIDE):
                tile = jnp.exp2(scores[group, :, i * BLOCK : (i + 1) * BLOCK] * SCALE2 - high)
                added += tile
                weights.append(tile.astype(jnp.bfloat16))
            total[...] = added
            acc[...] += jnp.dot(
                jnp.concatenate(weights, 1), gather(1, group), preferred_element_type=jnp.float32
            )
            return carry

        lax.fori_loop(0, groups, second, 0)
        result = (acc[...] / jnp.sum(total[...], axis=1, keepdims=True)).astype(jnp.bfloat16)
        here = slice(ahead + row * BLOCK, ahead + (row + 1) * BLOCK)
        for g in range(GROUP):
            out_ref[here, g * HD : (g + 1) * HD] = result[g * BLOCK : (g + 1) * BLOCK, :]


def attention(coords, block_list, q, first_row, n_rows, pieces, slots=()):
    rows = GROUP * BLOCK
    width = q.shape[1]
    tok = n_rows * BLOCK + (0 if slots else sum(piece.shape[0] for piece in pieces[1:]))
    kv_shape = (2, SLOTS * 512, HD)
    out_shape = [jax.ShapeDtypeStruct((tok, width), jnp.bfloat16)]
    if slots:
        out_shape.append(jax.ShapeDtypeStruct(kv_shape, jnp.bfloat16))
    return pl.pallas_call(
        functools.partial(attention_kernel, first_row, n_rows, slots),
        out_shape=out_shape,
        in_specs=[SMEM, SMEM, VMEM] + [VMEM] * len(pieces),
        out_specs=[VMEM] * len(out_shape),
        scratch_shapes=[
            pltpu.VMEM((KMAX // WIDE, rows, WIDE * BLOCK), jnp.float32),
            pltpu.VMEM((rows, HD), jnp.float32),
            pltpu.VMEM((rows, HD), jnp.float32),
            pltpu.VMEM((rows, HD), jnp.float32),
            pltpu.SMEM((n_rows, KMAX), jnp.int32),
        ],
        compiler_params=pltpu.CompilerParams(vmem_limit_bytes=ATTENTION_VMEM),
        cost_estimate=pl.CostEstimate(flops=ATT_FLOPS, bytes_accessed=0, transcendentals=0),
        name="attention",
    )(coords, block_list, q, *pieces)


def stack_kernel(groups, *refs):
    pieces, outs = refs[: -len(groups)], refs[-len(groups) :]
    for group, out in zip(groups, outs):
        at = 0
        for piece in (pieces[i] for i in group):
            n = piece.shape[0] if len(piece.shape) == 4 else 1
            out[at : at + n] = piece[...].reshape(n, *out.shape[1:])
            at += n


def stack(pieces, groups):
    sizes = [piece.shape[0] if piece.ndim == 4 else 1 for piece in pieces]
    shape, dtype = pieces[0].shape[-3:], pieces[0].dtype
    return pl.pallas_call(
        functools.partial(stack_kernel, groups),
        out_shape=[
            jax.ShapeDtypeStruct((sum(sizes[i] for i in group), *shape), dtype) for group in groups
        ],
        in_specs=[VMEM] * len(pieces),
        out_specs=[VMEM] * len(groups),
        compiler_params=pltpu.CompilerParams(vmem_limit_bytes=PROJECT_VMEM),
        cost_estimate=FREE,
        name="stack",
    )(*pieces)


def project_kernel(steps, coords, own_ref, near_ref, w_ref, w0a, w0b, w1a, w1b, *out_refs):
    core, yl, z = coords[2], coords[3], coords[4]

    def lanes(block):
        return pl.ds(pl.multiple_of(block * 512, 512), 512)

    for step, out_ref in zip(steps, out_refs):
        target = (z + step + NZ) % NZ
        mine = target // 4 == core
        part = lanes(target % 4)
        value = jnp.dot(
            own_ref[...], w_ref[:, lanes(yl * NZ + target)], preferred_element_type=jnp.float32
        )
        value += jnp.dot(
            near_ref[:, :NEAR_ROWS],
            jnp.where(mine, w0a[:, part], w0b[:, part]),
            preferred_element_type=jnp.float32,
        )
        value += jnp.dot(
            near_ref[:, NEAR_ROWS:],
            jnp.where(mine, w1a[:, part], w1b[:, part]),
            preferred_element_type=jnp.float32,
        )
        out_ref[...] = value.astype(jnp.bfloat16)


def project(coords, steps, own, near, weights, parts):
    rows = own.shape[0]
    count = len(steps)
    return pl.pallas_call(
        functools.partial(project_kernel, steps),
        out_shape=[jax.ShapeDtypeStruct((rows, 512), jnp.bfloat16)] * count,
        in_specs=[SMEM] + [VMEM] * 7,
        out_specs=[VMEM] * count,
        compiler_params=pltpu.CompilerParams(vmem_limit_bytes=PROJECT_VMEM),
        cost_estimate=FREE,
        name="project",
    )(coords, own, near, weights, *parts)


def shards(queries, keys_values, block_list, out_weight):
    ctx = lax.axis_index("ctx")
    tp = lax.axis_index("tp")
    coords = jnp.stack([ctx // 4, (ctx // 2) % 2, ctx % 2, tp // NZ, tp % NZ]).astype(jnp.int32)
    n_rows = queries.shape[0] // BLOCK // CHUNKS
    barrier = lax.optimization_barrier

    yl, z = tp // NZ, tp % NZ
    own = lax.dynamic_slice_in_dim(keys_values, (yl * 4 + z // 2) * HD, HD, 2)
    for_far = lax.dynamic_slice_in_dim(keys_values, ((1 - yl) * 4 + z // 2) * HD, HD, 2)
    far = send(for_far, "y_far")
    left = send(own, "x+")
    right = send(own, "x-")

    near_w, far_w = pick(coords, out_weight)
    far, left, right, near_w, far_w = barrier((far, left, right, near_w, far_w))
    near_part = send(near_w, "y_near")
    far_part = send(far_w, "y_far")
    one, four = stack([own, far, left, right], ((1, 2), (0, 1, 2, 3)))
    far_right = send(far, "x-")
    both = send(one, "x+")
    two_far = send(far_right, "x-")
    far_right_there, both = barrier((far_right, both))
    late = [both, far_right, two_far]
    pieces = [four, send(four, "core"), *late]
    pieces += [send(piece, "core") for piece in (both, far_right_there, two_far)]
    slots = ((0, 2, 12, 4), (1, 3, 13, 5), (14, 8), (6,), (10,), (15, 9), (7,), (11,))

    first, kv = attention(coords, block_list, queries, 0, n_rows, pieces, slots)
    attended = [first] + [
        attention(coords, block_list, queries, k * n_rows, n_rows, [kv])[0] for k in range(1, CHUNKS)
    ]
    near = [send(first, "y_near"), None]
    near_part, far_part, near[0], near[1] = barrier((near_part, far_part, near[0], attended[1]))
    near[1] = send(near[1], "y_near")
    near_other, far_other = send(near_part, "core"), send(far_part, "core")
    parts = [near_part, near_other, far_part, far_other]

    def add(*terms):
        return sum(t.astype(jnp.float32) for t in terms).astype(jnp.bfloat16)

    moves = ("z+", "z-")
    ways, moving = [], []
    for k in range(CHUNKS):
        orders = ((4, 3, 2, 1), (-3, -2, -1)) if k % 2 == 0 else ((3, 2, 1), (-4, -3, -2, -1))
        early = tuple(order[0] for order in orders)
        late = (*orders[0][1:], *orders[1][1:], 0)
        begun = project(coords, early, attended[k], near[k], out_weight, parts)
        moving.append([send(value, move) for value, move in zip(begun, moves)])
        partial = dict(zip(late, project(coords, late, attended[k], near[k], out_weight, parts)))
        ways.append((orders, partial))

    for step in range(1, 4):
        for k in range(CHUNKS):
            orders, partial = ways[k]
            for way, order in enumerate(orders):
                if step < len(order):
                    moving[k][way] = send(add(moving[k][way], partial[order[step]]), moves[way])
    results = [add(ways[k][1][0], *moving[k]) for k in range(CHUNKS)]
    return jnp.concatenate(results, 0)


def solution(mesh):
    in_specs = (P("ctx", "tp"), P(None, "ctx", None), P("ctx", None), P("tp", None))
    return jax.shard_map(
        shards, mesh=mesh, in_specs=in_specs, out_specs=P("ctx", "tp"), check_vma=False
    )
```

```python
import functools
import math

import jax
import jax.numpy as jnp
from jax import lax
from jax.experimental import pallas as pl
from jax.experimental.pallas import tpu as pltpu
from jax.sharding import PartitionSpec as P

HD = 128
BLOCK = 128
KMAX = 16
GROUP = 4
AXES = ("ctx", "tp")
NX, NYH, NC, NYL, NZ = 4, 2, 2, 2, 8
SLOTS = NX * NYH * NC
SCALE2 = HD ** (-0.5) * math.log2(math.e)
CHUNKS = 2
LOW = -1e30
NEAR_ROWS = 224
ATTENTION_VMEM = 14 * 2**20
PROJECT_VMEM = 8 * 2**20
WIDE = 4
ATT_FLOPS = 0
VMEM_LIMIT = 50 * 2**20
FREE = pl.CostEstimate(flops=0, bytes_accessed=0, transcendentals=0)


def pairs(move):
    out = []
    for x in range(NX):
        for y in range(4):
            for c in range(NC):
                for z in range(NZ):
                    x2, y2, c2, z2 = move(x, y, c, z)
                    x2, y2, c2, z2 = x2 % NX, y2 % 4, c2 % NC, z2 % NZ

                    def index(x, y, c, z):
                        return (x * 4 + (y // 2) * 2 + c) * 16 + (y % 2) * 8 + z

                    out.append((index(x, y, c, z), index(x2, y2, c2, z2)))
    return out


MOVES = {
    "x+": pairs(lambda x, y, c, z: (x + 1, y, c, z)),
    "x-": pairs(lambda x, y, c, z: (x - 1, y, c, z)),
    "z+": pairs(lambda x, y, c, z: (x, y, c, z + 1)),
    "z-": pairs(lambda x, y, c, z: (x, y, c, z - 1)),
    **{
        f"swing{sign}{parity}": pairs(
            lambda x, y, c, z: (x, y, c, z + (sign if (z + c) % 2 == parity else -sign))
        )
        for sign in (1, -1)
        for parity in (0, 1)
    },
    "core": pairs(lambda x, y, c, z: (x, y, c + 1, z)),
    "y_near": pairs(lambda x, y, c, z: (x, y ^ 1, c, z)),
    "y_far": pairs(lambda x, y, c, z: (x, 3 - y, c, z)),
}


def send(array, move):
    return lax.ppermute(array, AXES, MOVES[move])


SMEM = pl.BlockSpec(memory_space=pltpu.SMEM)
VMEM = pl.BlockSpec(memory_space=pltpu.VMEM)
HBM = pl.BlockSpec(memory_space=pltpu.HBM)


REACH = ((4, -2, 2, 0), (-3, 3, -1, 1))


def pick_kernel(coords, w_ref, near_w_ref, far_w_ref, sems):
    c, yl = coords[2], coords[3]
    copies = []
    for j in range(NZ // 2):
        there = pl.ds(pl.multiple_of(((1 - yl) * NZ + 2 * j + c) * 512, 512), 512)
        here = pl.ds(j * 512, 512)
        row = 0
        for i, out in enumerate((near_w_ref, far_w_ref)):
            rows = pl.ds(row, out.shape[0])
            copies.append(
                pltpu.make_async_copy(w_ref.at[rows, there], out.at[:, here], sems.at[2 * j + i])
            )
            row += out.shape[0]
    for copy in copies:
        copy.start()
    for copy in copies:
        copy.wait()


def pick(coords, weights):
    depth, full = weights.shape
    parts = [jax.ShapeDtypeStruct((n, full // 4), jnp.bfloat16) for n in (NEAR_ROWS, depth - NEAR_ROWS)]
    return pl.pallas_call(
        pick_kernel,
        out_shape=parts,
        in_specs=[SMEM, HBM],
        out_specs=[VMEM] * 2,
        scratch_shapes=[pltpu.SemaphoreType.DMA((NZ,))],
        compiler_params=pltpu.CompilerParams(vmem_limit_bytes=VMEM_LIMIT),
        cost_estimate=FREE,
        name="pick",
    )(coords, weights)


def attention_kernel(first_row, n_rows, slots, coords, block_list, q_ref, *refs):
    if slots:
        pieces, refs = refs[: len(slots)], refs[len(slots) :]
        out_ref, kv, scores, top, total, acc, placed = refs
        for piece, held in zip(pieces, slots):
            for i, slot in enumerate(held):
                kv[:, slot * 512 : (slot + 1) * 512, :] = piece[i] if len(held) > 1 else piece[...]
    else:
        kv, refs = refs[0], refs[1:]
        before, refs = refs[:-6], refs[-6:]
        out_ref, scores, top, total, acc, placed = refs
        done = 0
        for ref in before:
            out_ref[done : done + ref.shape[0], :] = ref[...]
            done += ref.shape[0]
    ahead = out_ref.shape[0] - n_rows * BLOCK
    x, yh, c = coords[0], coords[1], coords[2]

    counts = []
    for row in range(n_rows):

        def place(j, count):
            block = block_list[first_row + row, j]
            shard = jnp.maximum(block, 0) // 4
            slot = ((shard // 4 - x) % NX) * 4 + (((shard // 2) % 2 - yh) % 2) * 2 + (shard - c) % 2
            placed[row, j] = (slot * 4 + block % 4) * BLOCK
            return count + (block >= 0).astype(jnp.int32)

        counts.append(lax.fori_loop(0, KMAX, place, 0))

    for row in range(n_rows):
        count = counts[row]
        groups = (count + WIDE - 1) // WIDE

        def gather(which, group):
            tiles = []
            for i in range(WIDE):
                j = jnp.minimum(group * WIDE + i, count - 1)
                tiles.append(kv[which, pl.ds(pl.multiple_of(placed[row, j], BLOCK), BLOCK), :])
            return jnp.concatenate(tiles, 0)

        rows = slice((first_row + row) * BLOCK, (first_row + row + 1) * BLOCK)
        q = jnp.concatenate([q_ref[rows, g * HD : (g + 1) * HD] for g in range(GROUP)], 0)
        top[...] = jnp.full(top.shape, LOW, jnp.float32)

        def first(group, carry):
            s = lax.dot_general(
                q, gather(0, group), (((1,), (1,)), ((), ())), preferred_element_type=jnp.float32
            )
            high = top[...]
            for i in range(WIDE):
                tile = s[:, i * BLOCK : (i + 1) * BLOCK]
                if i:
                    tile = jnp.where(group * WIDE + i < count, tile, LOW)
                scores[group, :, i * BLOCK : (i + 1) * BLOCK] = tile
                high = jnp.maximum(high, tile)
            top[...] = high
            return carry

        lax.fori_loop(0, groups, first, 0)
        top[...] = jnp.broadcast_to(jnp.max(top[...], axis=1, keepdims=True) * SCALE2, top.shape)
        total[...] = jnp.zeros(total.shape, jnp.float32)
        acc[...] = jnp.zeros(acc.shape, jnp.float32)

        def second(group, carry):
            high = top[...]
            added, weights = total[...], []
            for i in range(WIDE):
                tile = jnp.exp2(scores[group, :, i * BLOCK : (i + 1) * BLOCK] * SCALE2 - high)
                added += tile
                weights.append(tile.astype(jnp.bfloat16))
            total[...] = added
            acc[...] += jnp.dot(
                jnp.concatenate(weights, 1), gather(1, group), preferred_element_type=jnp.float32
            )
            return carry

        lax.fori_loop(0, groups, second, 0)
        result = (acc[...] / jnp.sum(total[...], axis=1, keepdims=True)).astype(jnp.bfloat16)
        here = slice(ahead + row * BLOCK, ahead + (row + 1) * BLOCK)
        for g in range(GROUP):
            out_ref[here, g * HD : (g + 1) * HD] = result[g * BLOCK : (g + 1) * BLOCK, :]


def attention(coords, block_list, q, first_row, n_rows, pieces, slots=()):
    rows = GROUP * BLOCK
    width = q.shape[1]
    tok = n_rows * BLOCK + (0 if slots else sum(piece.shape[0] for piece in pieces[1:]))
    kv_shape = (2, SLOTS * 512, HD)
    out_shape = [jax.ShapeDtypeStruct((tok, width), jnp.bfloat16)]
    if slots:
        out_shape.append(jax.ShapeDtypeStruct(kv_shape, jnp.bfloat16))
    return pl.pallas_call(
        functools.partial(attention_kernel, first_row, n_rows, slots),
        out_shape=out_shape,
        in_specs=[SMEM, SMEM, VMEM] + [VMEM] * len(pieces),
        out_specs=[VMEM] * len(out_shape),
        scratch_shapes=[
            pltpu.VMEM((KMAX // WIDE, rows, WIDE * BLOCK), jnp.float32),
            pltpu.VMEM((rows, HD), jnp.float32),
            pltpu.VMEM((rows, HD), jnp.float32),
            pltpu.VMEM((rows, HD), jnp.float32),
            pltpu.SMEM((n_rows, KMAX), jnp.int32),
        ],
        compiler_params=pltpu.CompilerParams(vmem_limit_bytes=ATTENTION_VMEM),
        cost_estimate=pl.CostEstimate(flops=ATT_FLOPS, bytes_accessed=0, transcendentals=0),
        name="attention",
    )(coords, block_list, q, *pieces)


def stack_kernel(groups, *refs):
    pieces, outs = refs[: -len(groups)], refs[-len(groups) :]
    for group, out in zip(groups, outs):
        at = 0
        for piece in (pieces[i] for i in group):
            n = piece.shape[0] if len(piece.shape) == 4 else 1
            out[at : at + n] = piece[...].reshape(n, *out.shape[1:])
            at += n


def stack(pieces, groups):
    sizes = [piece.shape[0] if piece.ndim == 4 else 1 for piece in pieces]
    shape, dtype = pieces[0].shape[-3:], pieces[0].dtype
    return pl.pallas_call(
        functools.partial(stack_kernel, groups),
        out_shape=[
            jax.ShapeDtypeStruct((sum(sizes[i] for i in group), *shape), dtype) for group in groups
        ],
        in_specs=[VMEM] * len(pieces),
        out_specs=[VMEM] * len(groups),
        compiler_params=pltpu.CompilerParams(vmem_limit_bytes=PROJECT_VMEM),
        cost_estimate=FREE,
        name="stack",
    )(*pieces)


def project_kernel(steps, sign, coords, own_ref, near_ref, w_ref, *refs):
    out_refs = refs[-len(steps) :]
    parts = refs[: -len(steps)]
    c, yl, z = coords[2], coords[3], coords[4]
    odd = (z + c) % 2

    def lanes(block):
        return pl.ds(pl.multiple_of(block * 512, 512), 512)

    for (other, step), out_ref in zip(steps, out_refs):
        w0_ref, w1_ref = parts[2 * other : 2 * other + 2] if len(parts) > 2 else parts
        reach = jnp.where(odd == other, REACH[0][step], REACH[1][step])
        target = (z + sign * reach + NZ) % NZ
        part = lanes(target // 2)
        value = jnp.dot(
            own_ref[...], w_ref[:, lanes(yl * NZ + target)], preferred_element_type=jnp.float32
        )
        value += jnp.dot(
            near_ref[:, :NEAR_ROWS], w0_ref[:, part], preferred_element_type=jnp.float32
        )
        value += jnp.dot(
            near_ref[:, NEAR_ROWS:], w1_ref[:, part], preferred_element_type=jnp.float32
        )
        out_ref[...] = value.astype(jnp.bfloat16)


def project(coords, steps, sign, own, near, weights, parts):
    count = len(steps)
    return pl.pallas_call(
        functools.partial(project_kernel, steps, sign),
        out_shape=[jax.ShapeDtypeStruct((own.shape[0], 512), jnp.bfloat16)] * count,
        in_specs=[SMEM] + [VMEM] * (3 + len(parts)),
        out_specs=[VMEM] * count,
        compiler_params=pltpu.CompilerParams(vmem_limit_bytes=PROJECT_VMEM),
        cost_estimate=FREE,
        name="project",
    )(coords, own, near, weights, *parts)


def shards(queries, keys_values, block_list, out_weight):
    ctx = lax.axis_index("ctx")
    tp = lax.axis_index("tp")
    coords = jnp.stack([ctx // 4, (ctx // 2) % 2, ctx % 2, tp // NZ, tp % NZ]).astype(jnp.int32)
    n_rows = queries.shape[0] // BLOCK // CHUNKS
    barrier = lax.optimization_barrier

    yl, z = tp // NZ, tp % NZ
    own = lax.dynamic_slice_in_dim(keys_values, (yl * 4 + z // 2) * HD, HD, 2)
    for_far = lax.dynamic_slice_in_dim(keys_values, ((1 - yl) * 4 + z // 2) * HD, HD, 2)
    far = send(for_far, "y_far")
    left = send(own, "x+")
    right = send(own, "x-")

    near_w, far_w = pick(coords, out_weight)
    far, left, right, near_w, far_w = barrier((far, left, right, near_w, far_w))
    near_part = send(near_w, "y_near")
    far_part = send(far_w, "y_far")
    one, four = stack([own, far, left, right], ((1, 2), (0, 1, 2, 3)))
    far_right = send(far, "x-")
    both = send(one, "x+")
    two_far = send(far_right, "x-")
    far_right_there, both = barrier((far_right, both))
    late = [both, far_right, two_far]
    pieces = [four, send(four, "core"), *late]
    pieces += [send(piece, "core") for piece in (both, far_right_there, two_far)]
    slots = ((0, 2, 12, 4), (1, 3, 13, 5), (14, 8), (6,), (10,), (15, 9), (7,), (11,))

    first, kv = attention(coords, block_list, queries, 0, n_rows, pieces, slots)
    attended = [first] + [
        attention(coords, block_list, queries, k * n_rows, n_rows, [kv])[0] for k in range(1, CHUNKS)
    ]
    near = [send(first, "y_near"), None]
    near_part, far_part, near[0], near[1] = barrier((near_part, far_part, near[0], attended[1]))
    near[1] = send(near[1], "y_near")
    near_other, far_other = send(near_part, "core"), send(far_part, "core")
    same, others = (near_part, far_part), (near_other, far_other)

    def add(*terms):
        return sum(t.astype(jnp.float32) for t in terms).astype(jnp.bfloat16)

    signs = (1, -1)
    even = (ctx + z) % 2 == 0
    partial, moving = [], []
    for k in range(CHUNKS):
        of_chunk = (signs[k], attended[k], near[k], out_weight)
        if k:
            begun = project(coords, ((0, 0), (1, 0)), *of_chunk, (*same, *others))
        else:
            begun = list(project(coords, ((0, 0),), *of_chunk, same))
            begun += project(coords, ((1, 0),), *of_chunk, others)
            near[1], begun[1] = barrier((near[1], begun[1]))
        moving.append([send(begun[i], f"swing{signs[k]}{i}") for i in range(2)])
        steps = tuple((i, step) for step in (1, 2, 3) for i in range(2))
        partial.append(dict(zip(steps, project(coords, steps, *of_chunk, (*same, *others)))))
    for step in (1, 2):
        for k in range(CHUNKS):
            for i in range(2):
                value = add(moving[k][i], partial[k][i, step])
                moving[k][i] = send(value, f"swing{signs[k]}{(step + i) % 2}")
    results = []
    for k in range(CHUNKS):
        last = [add(moving[k][i], partial[k][i, 3]) for i in range(2)]
        held, going = jnp.where(even, last[0], last[1]), jnp.where(even, last[1], last[0])
        results.append(add(held, send(going, "z+" if signs[k] > 0 else "z-")))
    return jnp.concatenate(results, 0)


def solution(mesh):
    in_specs = (P("ctx", "tp"), P(None, "ctx", None), P("ctx", None), P("tp", None))
    return jax.shard_map(
        shards, mesh=mesh, in_specs=in_specs, out_specs=P("ctx", "tp"), check_vma=False
    )
```

```python
import functools
import math

import jax
import jax.numpy as jnp
from jax import lax
from jax.experimental import pallas as pl
from jax.experimental.pallas import tpu as pltpu
from jax.sharding import PartitionSpec as P

HD = 128
BLOCK = 128
KMAX = 16
GROUP = 4
AXES = ("ctx", "tp")
NX, NYH, NC, NYL, NZ = 4, 2, 2, 2, 8
SLOTS = NX * NYH * NC
SCALE2 = HD ** (-0.5) * math.log2(math.e)
CHUNKS = 2
LOW = -1e30
NEAR_ROWS = 208
ATTENTION_VMEM = 14 * 2**20
PROJECT_VMEM = 8 * 2**20
WIDE = 4
ATT_FLOPS = 0
VMEM_LIMIT = 50 * 2**20
FREE = pl.CostEstimate(flops=0, bytes_accessed=0, transcendentals=0)


def pairs(move):
    out = []
    for x in range(NX):
        for y in range(4):
            for c in range(NC):
                for z in range(NZ):
                    x2, y2, c2, z2 = move(x, y, c, z)
                    x2, y2, c2, z2 = x2 % NX, y2 % 4, c2 % NC, z2 % NZ

                    def index(x, y, c, z):
                        return (x * 4 + (y // 2) * 2 + c) * 16 + (y % 2) * 8 + z

                    out.append((index(x, y, c, z), index(x2, y2, c2, z2)))
    return out


MOVES = {
    "x+": pairs(lambda x, y, c, z: (x + 1, y, c, z)),
    "x-": pairs(lambda x, y, c, z: (x - 1, y, c, z)),
    "z+": pairs(lambda x, y, c, z: (x, y, c, z + 1)),
    "z-": pairs(lambda x, y, c, z: (x, y, c, z - 1)),
    "core": pairs(lambda x, y, c, z: (x, y, c + 1, z)),
    "y_near": pairs(lambda x, y, c, z: (x, y ^ 1, c, z)),
    "y_far": pairs(lambda x, y, c, z: (x, 3 - y, c, z)),
}


def send(array, move):
    return lax.ppermute(array, AXES, MOVES[move])


SMEM = pl.BlockSpec(memory_space=pltpu.SMEM)
VMEM = pl.BlockSpec(memory_space=pltpu.VMEM)
HBM = pl.BlockSpec(memory_space=pltpu.HBM)


def pick_kernel(coords, w_ref, near_w_ref, far_w_ref, sems):
    c, yl = coords[2], coords[3]
    columns = near_w_ref.shape[1]
    near_rows, far_rows = near_w_ref.shape[0], far_w_ref.shape[0]
    there = pl.ds(pl.multiple_of(((1 - yl) * 2 + c) * columns, columns), columns)
    copies = [
        pltpu.make_async_copy(w_ref.at[pl.ds(0, near_rows), there], near_w_ref, sems.at[0]),
        pltpu.make_async_copy(w_ref.at[pl.ds(near_rows, far_rows), there], far_w_ref, sems.at[1]),
    ]
    for copy in copies:
        copy.start()
    for copy in copies:
        copy.wait()


def pick(coords, weights):
    depth, full = weights.shape
    parts = [jax.ShapeDtypeStruct((n, full // 4), jnp.bfloat16) for n in (NEAR_ROWS, depth - NEAR_ROWS)]
    return pl.pallas_call(
        pick_kernel,
        out_shape=parts,
        in_specs=[SMEM, HBM],
        out_specs=[VMEM] * 2,
        scratch_shapes=[pltpu.SemaphoreType.DMA((2,))],
        compiler_params=pltpu.CompilerParams(vmem_limit_bytes=VMEM_LIMIT),
        cost_estimate=FREE,
        name="pick",
    )(coords, weights)


def attention_kernel(first_row, n_rows, slots, coords, block_list, q_ref, *refs):
    if slots:
        pieces, refs = refs[: len(slots)], refs[len(slots) :]
        out_ref, kv, scores, top, total, acc, placed = refs
        for piece, held in zip(pieces, slots):
            for i, slot in enumerate(held):
                kv[:, slot * 512 : (slot + 1) * 512, :] = piece[i] if len(held) > 1 else piece[...]
    else:
        kv, refs = refs[0], refs[1:]
        before, refs = refs[:-6], refs[-6:]
        out_ref, scores, top, total, acc, placed = refs
        done = 0
        for ref in before:
            out_ref[done : done + ref.shape[0], :] = ref[...]
            done += ref.shape[0]
    ahead = out_ref.shape[0] - n_rows * BLOCK
    x, yh, c = coords[0], coords[1], coords[2]

    counts = []
    for row in range(n_rows):

        def place(j, count):
            block = block_list[first_row + row, j]
            shard = jnp.maximum(block, 0) // 4
            slot = ((shard // 4 - x) % NX) * 4 + (((shard // 2) % 2 - yh) % 2) * 2 + (shard - c) % 2
            placed[row, j] = (slot * 4 + block % 4) * BLOCK
            return count + (block >= 0).astype(jnp.int32)

        counts.append(lax.fori_loop(0, KMAX, place, 0))

    for row in range(n_rows):
        count = counts[row]
        groups = (count + WIDE - 1) // WIDE

        def gather(which, group):
            tiles = []
            for i in range(WIDE):
                j = jnp.minimum(group * WIDE + i, count - 1)
                tiles.append(kv[which, pl.ds(pl.multiple_of(placed[row, j], BLOCK), BLOCK), :])
            return jnp.concatenate(tiles, 0)

        rows = slice((first_row + row) * BLOCK, (first_row + row + 1) * BLOCK)
        q = jnp.concatenate([q_ref[rows, g * HD : (g + 1) * HD] for g in range(GROUP)], 0)
        top[...] = jnp.full(top.shape, LOW, jnp.float32)

        def first(group, carry):
            s = lax.dot_general(
                q, gather(0, group), (((1,), (1,)), ((), ())), preferred_element_type=jnp.float32
            )
            high = top[...]
            for i in range(WIDE):
                tile = s[:, i * BLOCK : (i + 1) * BLOCK]
                if i:
                    tile = jnp.where(group * WIDE + i < count, tile, LOW)
                scores[group, :, i * BLOCK : (i + 1) * BLOCK] = tile
                high = jnp.maximum(high, tile)
            top[...] = high
            return carry

        lax.fori_loop(0, groups, first, 0)
        top[...] = jnp.broadcast_to(jnp.max(top[...], axis=1, keepdims=True) * SCALE2, top.shape)
        total[...] = jnp.zeros(total.shape, jnp.float32)
        acc[...] = jnp.zeros(acc.shape, jnp.float32)

        def second(group, carry):
            high = top[...]
            added, weights = total[...], []
            for i in range(WIDE):
                tile = jnp.exp2(scores[group, :, i * BLOCK : (i + 1) * BLOCK] * SCALE2 - high)
                added += tile
                weights.append(tile.astype(jnp.bfloat16))
            total[...] = added
            acc[...] += jnp.dot(
                jnp.concatenate(weights, 1), gather(1, group), preferred_element_type=jnp.float32
            )
            return carry

        lax.fori_loop(0, groups, second, 0)
        result = (acc[...] / jnp.sum(total[...], axis=1, keepdims=True)).astype(jnp.bfloat16)
        here = slice(ahead + row * BLOCK, ahead + (row + 1) * BLOCK)
        for g in range(GROUP):
            out_ref[here, g * HD : (g + 1) * HD] = result[g * BLOCK : (g + 1) * BLOCK, :]


def attention(coords, block_list, q, first_row, n_rows, pieces, slots=()):
    rows = GROUP * BLOCK
    width = q.shape[1]
    tok = n_rows * BLOCK + (0 if slots else sum(piece.shape[0] for piece in pieces[1:]))
    kv_shape = (2, SLOTS * 512, HD)
    out_shape = [jax.ShapeDtypeStruct((tok, width), jnp.bfloat16)]
    if slots:
        out_shape.append(jax.ShapeDtypeStruct(kv_shape, jnp.bfloat16))
    return pl.pallas_call(
        functools.partial(attention_kernel, first_row, n_rows, slots),
        out_shape=out_shape,
        in_specs=[SMEM, SMEM, VMEM] + [VMEM] * len(pieces),
        out_specs=[VMEM] * len(out_shape),
        scratch_shapes=[
            pltpu.VMEM((KMAX // WIDE, rows, WIDE * BLOCK), jnp.float32),
            pltpu.VMEM((rows, HD), jnp.float32),
            pltpu.VMEM((rows, HD), jnp.float32),
            pltpu.VMEM((rows, HD), jnp.float32),
            pltpu.SMEM((n_rows, KMAX), jnp.int32),
        ],
        compiler_params=pltpu.CompilerParams(vmem_limit_bytes=ATTENTION_VMEM),
        cost_estimate=pl.CostEstimate(flops=ATT_FLOPS, bytes_accessed=0, transcendentals=0),
        name="attention",
    )(coords, block_list, q, *pieces)


def stack_kernel(groups, *refs):
    pieces, outs = refs[: -len(groups)], refs[-len(groups) :]
    for group, out in zip(groups, outs):
        at = 0
        for piece in (pieces[i] for i in group):
            n = piece.shape[0] if len(piece.shape) == 4 else 1
            out[at : at + n] = piece[...].reshape(n, *out.shape[1:])
            at += n


def stack(pieces, groups):
    sizes = [piece.shape[0] if piece.ndim == 4 else 1 for piece in pieces]
    shape, dtype = pieces[0].shape[-3:], pieces[0].dtype
    return pl.pallas_call(
        functools.partial(stack_kernel, groups),
        out_shape=[
            jax.ShapeDtypeStruct((sum(sizes[i] for i in group), *shape), dtype) for group in groups
        ],
        in_specs=[VMEM] * len(pieces),
        out_specs=[VMEM] * len(groups),
        compiler_params=pltpu.CompilerParams(vmem_limit_bytes=PROJECT_VMEM),
        cost_estimate=FREE,
        name="stack",
    )(*pieces)


def project_kernel(steps, coords, own_ref, near_ref, w_ref, w0a, w0b, w1a, w1b, *out_refs):
    core, yl, z = coords[2], coords[3], coords[4]

    def lanes(block):
        return pl.ds(pl.multiple_of(block * 512, 512), 512)

    for step, out_ref in zip(steps, out_refs):
        target = (z + step + NZ) % NZ
        mine = target // 4 == core
        part = lanes(target % 4)
        value = jnp.dot(
            own_ref[...], w_ref[:, lanes(yl * NZ + target)], preferred_element_type=jnp.float32
        )
        value += jnp.dot(
            near_ref[:, :NEAR_ROWS],
            jnp.where(mine, w0a[:, part], w0b[:, part]),
            preferred_element_type=jnp.float32,
        )
        value += jnp.dot(
            near_ref[:, NEAR_ROWS:],
            jnp.where(mine, w1a[:, part], w1b[:, part]),
            preferred_element_type=jnp.float32,
        )
        out_ref[...] = value.astype(jnp.bfloat16)


def project(coords, steps, own, near, weights, parts):
    rows = own.shape[0]
    count = len(steps)
    return pl.pallas_call(
        functools.partial(project_kernel, steps),
        out_shape=[jax.ShapeDtypeStruct((rows, 512), jnp.bfloat16)] * count,
        in_specs=[SMEM] + [VMEM] * 7,
        out_specs=[VMEM] * count,
        compiler_params=pltpu.CompilerParams(vmem_limit_bytes=PROJECT_VMEM),
        cost_estimate=FREE,
        name="project",
    )(coords, own, near, weights, *parts)


def shards(queries, keys_values, block_list, out_weight):
    ctx = lax.axis_index("ctx")
    tp = lax.axis_index("tp")
    coords = jnp.stack([ctx // 4, (ctx // 2) % 2, ctx % 2, tp // NZ, tp % NZ]).astype(jnp.int32)
    n_rows = queries.shape[0] // BLOCK // CHUNKS
    barrier = lax.optimization_barrier

    yl, z = tp // NZ, tp % NZ
    own = lax.dynamic_slice_in_dim(keys_values, (yl * 4 + z // 2) * HD, HD, 2)
    for_far = lax.dynamic_slice_in_dim(keys_values, ((1 - yl) * 4 + z // 2) * HD, HD, 2)
    far = send(for_far, "y_far")
    left = send(own, "x+")
    right = send(own, "x-")

    near_w, far_w = pick(coords, out_weight)
    far, left, right, near_w, far_w = barrier((far, left, right, near_w, far_w))
    near_part = send(near_w, "y_near")
    far_part = send(far_w, "y_far")
    one, four = stack([own, far, left, right], ((1, 2), (0, 1, 2, 3)))
    far_right = send(far, "x-")
    both = send(one, "x+")
    two_far = send(far_right, "x-")
    (pair,) = stack([far_right, two_far], ((0, 1),))
    pieces = [four, send(four, "core"), both, send(both, "core"), pair, send(pair, "core")]
    slots = ((0, 2, 12, 4), (1, 3, 13, 5), (14, 8), (15, 9), (6, 10), (7, 11))

    first, kv = attention(coords, block_list, queries, 0, n_rows, pieces, slots)
    attended = [first] + [
        attention(coords, block_list, queries, k * n_rows, n_rows, [kv])[0] for k in range(1, CHUNKS)
    ]
    near = [send(first, "y_near"), None]
    near_part, far_part, near[0], near[1] = barrier((near_part, far_part, near[0], attended[1]))
    near[1] = send(near[1], "y_near")
    near_other, far_other = send(near_part, "core"), send(far_part, "core")
    parts = [near_part, near_other, far_part, far_other]

    def add(*terms):
        return sum(t.astype(jnp.float32) for t in terms).astype(jnp.bfloat16)

    moves = ("z+", "z-")
    ways, moving = [], []
    for k in range(CHUNKS):
        orders = ((4, 3, 2, 1), (-3, -2, -1)) if k % 2 == 0 else ((3, 2, 1), (-4, -3, -2, -1))
        early = tuple(order[0] for order in orders)
        late = (*orders[0][1:], *orders[1][1:], 0)
        begun = project(coords, early, attended[k], near[k], out_weight, parts)
        moving.append([send(value, move) for value, move in zip(begun, moves)])
        partial = dict(zip(late, project(coords, late, attended[k], near[k], out_weight, parts)))
        ways.append((orders, partial))

    for step in range(1, 4):
        for k in range(CHUNKS):
            orders, partial = ways[k]
            for way, order in enumerate(orders):
                if step < len(order):
                    moving[k][way] = send(add(moving[k][way], partial[order[step]]), moves[way])
    results = [add(ways[k][1][0], *moving[k]) for k in range(CHUNKS)]
    return jnp.concatenate(results, 0)


def solution(mesh):
    in_specs = (P("ctx", "tp"), P(None, "ctx", None), P("ctx", None), P("tp", None))
    return jax.shard_map(
        shards, mesh=mesh, in_specs=in_specs, out_specs=P("ctx", "tp"), check_vma=False
    )
```

```python
import functools
import math

import jax
import jax.numpy as jnp
from jax import lax
from jax.experimental import pallas as pl
from jax.experimental.pallas import tpu as pltpu
from jax.sharding import PartitionSpec as P

HD = 128
BLOCK = 128
KMAX = 16
GROUP = 4
AXES = ("ctx", "tp")
NX, NYH, NC, NYL, NZ = 4, 2, 2, 2, 8
SLOTS = NX * NYH * NC
SCALE2 = HD ** (-0.5) * math.log2(math.e)
CHUNKS = 2
LOW = -1e30
NEAR_ROWS = 208
ATTENTION_VMEM = 14 * 2**20
PROJECT_VMEM = 8 * 2**20
WIDE = 4
ATT_FLOPS = 0
VMEM_LIMIT = 50 * 2**20
FREE = pl.CostEstimate(flops=0, bytes_accessed=0, transcendentals=0)


def pairs(move):
    out = []
    for x in range(NX):
        for y in range(4):
            for c in range(NC):
                for z in range(NZ):
                    x2, y2, c2, z2 = move(x, y, c, z)
                    x2, y2, c2, z2 = x2 % NX, y2 % 4, c2 % NC, z2 % NZ

                    def index(x, y, c, z):
                        return (x * 4 + (y // 2) * 2 + c) * 16 + (y % 2) * 8 + z

                    out.append((index(x, y, c, z), index(x2, y2, c2, z2)))
    return out


MOVES = {
    "x+": pairs(lambda x, y, c, z: (x + 1, y, c, z)),
    "x-": pairs(lambda x, y, c, z: (x - 1, y, c, z)),
    "z+": pairs(lambda x, y, c, z: (x, y, c, z + 1)),
    "z-": pairs(lambda x, y, c, z: (x, y, c, z - 1)),
    "core": pairs(lambda x, y, c, z: (x, y, c + 1, z)),
    "y_near": pairs(lambda x, y, c, z: (x, y ^ 1, c, z)),
    "y_far": pairs(lambda x, y, c, z: (x, 3 - y, c, z)),
}


def send(array, move):
    return lax.ppermute(array, AXES, MOVES[move])


SMEM = pl.BlockSpec(memory_space=pltpu.SMEM)
VMEM = pl.BlockSpec(memory_space=pltpu.VMEM)
HBM = pl.BlockSpec(memory_space=pltpu.HBM)


def pick_kernel(coords, w_ref, near_w_ref, far_w_ref, sems):
    c, yl = coords[2], coords[3]
    columns = near_w_ref.shape[1]
    near_rows, far_rows = near_w_ref.shape[0], far_w_ref.shape[0]
    there = pl.ds(pl.multiple_of(((1 - yl) * 2 + c) * columns, columns), columns)
    copies = [
        pltpu.make_async_copy(w_ref.at[pl.ds(0, near_rows), there], near_w_ref, sems.at[0]),
        pltpu.make_async_copy(w_ref.at[pl.ds(near_rows, far_rows), there], far_w_ref, sems.at[1]),
    ]
    for copy in copies:
        copy.start()
    for copy in copies:
        copy.wait()


def pick(coords, weights):
    depth, full = weights.shape
    parts = [jax.ShapeDtypeStruct((n, full // 4), jnp.bfloat16) for n in (NEAR_ROWS, depth - NEAR_ROWS)]
    return pl.pallas_call(
        pick_kernel,
        out_shape=parts,
        in_specs=[SMEM, HBM],
        out_specs=[VMEM] * 2,
        scratch_shapes=[pltpu.SemaphoreType.DMA((2,))],
        compiler_params=pltpu.CompilerParams(vmem_limit_bytes=VMEM_LIMIT),
        cost_estimate=FREE,
        name="pick",
    )(coords, weights)


def attention_kernel(first_row, n_rows, slots, coords, block_list, q_ref, *refs):
    if slots:
        pieces, refs = refs[: len(slots)], refs[len(slots) :]
        out_ref, kv, scores, top, total, acc, placed = refs
        for piece, held in zip(pieces, slots):
            for i, slot in enumerate(held):
                kv[:, slot * 512 : (slot + 1) * 512, :] = piece[i] if len(held) > 1 else piece[...]
    else:
        kv, refs = refs[0], refs[1:]
        before, refs = refs[:-6], refs[-6:]
        out_ref, scores, top, total, acc, placed = refs
        done = 0
        for ref in before:
            out_ref[done : done + ref.shape[0], :] = ref[...]
            done += ref.shape[0]
    ahead = out_ref.shape[0] - n_rows * BLOCK
    x, yh, c = coords[0], coords[1], coords[2]

    counts = []
    for row in range(n_rows):

        def place(j, count):
            block = block_list[first_row + row, j]
            shard = jnp.maximum(block, 0) // 4
            slot = ((shard // 4 - x) % NX) * 4 + (((shard // 2) % 2 - yh) % 2) * 2 + (shard - c) % 2
            placed[row, j] = (slot * 4 + block % 4) * BLOCK
            return count + (block >= 0).astype(jnp.int32)

        counts.append(lax.fori_loop(0, KMAX, place, 0))

    for row in range(n_rows):
        count = counts[row]
        groups = (count + WIDE - 1) // WIDE

        def gather(which, group):
            tiles = []
            for i in range(WIDE):
                j = jnp.minimum(group * WIDE + i, count - 1)
                tiles.append(kv[which, pl.ds(pl.multiple_of(placed[row, j], BLOCK), BLOCK), :])
            return jnp.concatenate(tiles, 0)

        rows = slice((first_row + row) * BLOCK, (first_row + row + 1) * BLOCK)
        q = jnp.concatenate([q_ref[rows, g * HD : (g + 1) * HD] for g in range(GROUP)], 0)
        top[...] = jnp.full(top.shape, LOW, jnp.float32)

        def first(group, carry):
            s = lax.dot_general(
                q, gather(0, group), (((1,), (1,)), ((), ())), preferred_element_type=jnp.float32
            )
            high = top[...]
            for i in range(WIDE):
                tile = s[:, i * BLOCK : (i + 1) * BLOCK]
                if i:
                    tile = jnp.where(group * WIDE + i < count, tile, LOW)
                scores[group, :, i * BLOCK : (i + 1) * BLOCK] = tile
                high = jnp.maximum(high, tile)
            top[...] = high
            return carry

        lax.fori_loop(0, groups, first, 0)
        top[...] = jnp.broadcast_to(jnp.max(top[...], axis=1, keepdims=True) * SCALE2, top.shape)
        total[...] = jnp.zeros(total.shape, jnp.float32)
        acc[...] = jnp.zeros(acc.shape, jnp.float32)

        def second(group, carry):
            high = top[...]
            added, weights = total[...], []
            for i in range(WIDE):
                tile = jnp.exp2(scores[group, :, i * BLOCK : (i + 1) * BLOCK] * SCALE2 - high)
                added += tile
                weights.append(tile.astype(jnp.bfloat16))
            total[...] = added
            acc[...] += jnp.dot(
                jnp.concatenate(weights, 1), gather(1, group), preferred_element_type=jnp.float32
            )
            return carry

        lax.fori_loop(0, groups, second, 0)
        result = (acc[...] / jnp.sum(total[...], axis=1, keepdims=True)).astype(jnp.bfloat16)
        here = slice(ahead + row * BLOCK, ahead + (row + 1) * BLOCK)
        for g in range(GROUP):
            out_ref[here, g * HD : (g + 1) * HD] = result[g * BLOCK : (g + 1) * BLOCK, :]


def attention(coords, block_list, q, first_row, n_rows, pieces, slots=()):
    rows = GROUP * BLOCK
    width = q.shape[1]
    tok = n_rows * BLOCK + (0 if slots else sum(piece.shape[0] for piece in pieces[1:]))
    kv_shape = (2, SLOTS * 512, HD)
    out_shape = [jax.ShapeDtypeStruct((tok, width), jnp.bfloat16)]
    if slots:
        out_shape.append(jax.ShapeDtypeStruct(kv_shape, jnp.bfloat16))
    return pl.pallas_call(
        functools.partial(attention_kernel, first_row, n_rows, slots),
        out_shape=out_shape,
        in_specs=[SMEM, SMEM, VMEM] + [VMEM] * len(pieces),
        out_specs=[VMEM] * len(out_shape),
        scratch_shapes=[
            pltpu.VMEM((KMAX // WIDE, rows, WIDE * BLOCK), jnp.float32),
            pltpu.VMEM((rows, HD), jnp.float32),
            pltpu.VMEM((rows, HD), jnp.float32),
            pltpu.VMEM((rows, HD), jnp.float32),
            pltpu.SMEM((n_rows, KMAX), jnp.int32),
        ],
        compiler_params=pltpu.CompilerParams(vmem_limit_bytes=ATTENTION_VMEM),
        cost_estimate=pl.CostEstimate(flops=ATT_FLOPS, bytes_accessed=0, transcendentals=0),
        name="attention",
    )(coords, block_list, q, *pieces)


def stack_kernel(groups, *refs):
    pieces, outs = refs[: -len(groups)], refs[-len(groups) :]
    for group, out in zip(groups, outs):
        at = 0
        for piece in (pieces[i] for i in group):
            n = piece.shape[0] if len(piece.shape) == 4 else 1
            out[at : at + n] = piece[...].reshape(n, *out.shape[1:])
            at += n


def stack(pieces, groups):
    sizes = [piece.shape[0] if piece.ndim == 4 else 1 for piece in pieces]
    shape, dtype = pieces[0].shape[-3:], pieces[0].dtype
    return pl.pallas_call(
        functools.partial(stack_kernel, groups),
        out_shape=[
            jax.ShapeDtypeStruct((sum(sizes[i] for i in group), *shape), dtype) for group in groups
        ],
        in_specs=[VMEM] * len(pieces),
        out_specs=[VMEM] * len(groups),
        compiler_params=pltpu.CompilerParams(vmem_limit_bytes=PROJECT_VMEM),
        cost_estimate=FREE,
        name="stack",
    )(*pieces)


def project_kernel(steps, coords, own_ref, near_ref, w_ref, w0a, w0b, w1a, w1b, *out_refs):
    core, yl, z = coords[2], coords[3], coords[4]

    def lanes(block):
        return pl.ds(pl.multiple_of(block * 512, 512), 512)

    for step, out_ref in zip(steps, out_refs):
        target = (z + step + NZ) % NZ
        mine = target // 4 == core
        part = lanes(target % 4)
        value = jnp.dot(
            own_ref[...], w_ref[:, lanes(yl * NZ + target)], preferred_element_type=jnp.float32
        )
        value += jnp.dot(
            near_ref[:, :NEAR_ROWS],
            jnp.where(mine, w0a[:, part], w0b[:, part]),
            preferred_element_type=jnp.float32,
        )
        value += jnp.dot(
            near_ref[:, NEAR_ROWS:],
            jnp.where(mine, w1a[:, part], w1b[:, part]),
            preferred_element_type=jnp.float32,
        )
        out_ref[...] = value.astype(jnp.bfloat16)


def project(coords, steps, own, near, weights, parts):
    rows = own.shape[0]
    count = len(steps)
    return pl.pallas_call(
        functools.partial(project_kernel, steps),
        out_shape=[jax.ShapeDtypeStruct((rows, 512), jnp.bfloat16)] * count,
        in_specs=[SMEM] + [VMEM] * 7,
        out_specs=[VMEM] * count,
        compiler_params=pltpu.CompilerParams(vmem_limit_bytes=PROJECT_VMEM),
        cost_estimate=FREE,
        name="project",
    )(coords, own, near, weights, *parts)


def shards(queries, keys_values, block_list, out_weight):
    ctx = lax.axis_index("ctx")
    tp = lax.axis_index("tp")
    coords = jnp.stack([ctx // 4, (ctx // 2) % 2, ctx % 2, tp // NZ, tp % NZ]).astype(jnp.int32)
    n_rows = queries.shape[0] // BLOCK // CHUNKS
    barrier = lax.optimization_barrier

    yl, z = tp // NZ, tp % NZ
    own = lax.dynamic_slice_in_dim(keys_values, (yl * 4 + z // 2) * HD, HD, 2)
    for_far = lax.dynamic_slice_in_dim(keys_values, ((1 - yl) * 4 + z // 2) * HD, HD, 2)
    far = send(for_far, "y_far")
    left = send(own, "x+")
    right = send(own, "x-")

    near_w, far_w = pick(coords, out_weight)
    far, left, right, near_w, far_w = barrier((far, left, right, near_w, far_w))
    near_part = send(near_w, "y_near")
    far_part = send(far_w, "y_far")
    one, four = stack([own, far, left, right], ((1, 2), (0, 1, 2, 3)))
    far_right = send(far, "x-")
    both = send(one, "x+")
    two_far = send(far_right, "x-")
    (pair,) = stack([far_right, two_far], ((0, 1),))
    pieces = [four, send(four, "core"), both, send(both, "core"), pair, send(pair, "core")]
    slots = ((0, 2, 12, 4), (1, 3, 13, 5), (14, 8), (15, 9), (6, 10), (7, 11))

    first, kv = attention(coords, block_list, queries, 0, n_rows, pieces, slots)
    attended = [first] + [
        attention(coords, block_list, queries, k * n_rows, n_rows, [kv])[0] for k in range(1, CHUNKS)
    ]
    near = [send(first, "y_near"), None]
    near_part, far_part, near[0], near[1] = barrier((near_part, far_part, near[0], attended[1]))
    near[1] = send(near[1], "y_near")
    near_other, far_other = send(near_part, "core"), send(far_part, "core")
    parts = [near_part, near_other, far_part, far_other]

    def add(*terms):
        return sum(t.astype(jnp.float32) for t in terms).astype(jnp.bfloat16)

    moves = ("z+", "z-")
    ways, moving = [], []
    for k in range(CHUNKS):
        orders = ((4, 3, 2, 1), (-3, -2, -1)) if k % 2 == 0 else ((3, 2, 1), (-4, -3, -2, -1))
        early = tuple(order[0] for order in orders)
        late = (*orders[0][1:], *orders[1][1:], 0)
        begun = project(coords, early, attended[k], near[k], out_weight, parts)
        moving.append([send(value, move) for value, move in zip(begun, moves)])
        held = near[k]
        if k:
            held, moving[0][0], moving[0][1] = barrier((held, moving[0][0], moving[0][1]))
        partial = dict(zip(late, project(coords, late, attended[k], held, out_weight, parts)))
        ways.append((orders, partial))

    for step in range(1, 4):
        for k in range(CHUNKS):
            orders, partial = ways[k]
            for way, order in enumerate(orders):
                if step < len(order):
                    moving[k][way] = send(add(moving[k][way], partial[order[step]]), moves[way])
    results = [add(ways[k][1][0], *moving[k]) for k in range(CHUNKS)]
    return jnp.concatenate(results, 0)


def solution(mesh):
    in_specs = (P("ctx", "tp"), P(None, "ctx", None), P("ctx", None), P("tp", None))
    return jax.shard_map(
        shards, mesh=mesh, in_specs=in_specs, out_specs=P("ctx", "tp"), check_vma=False
    )
```
